256 devices in a mesh: pb: 8 (over z_lo, core), pa: 32 (over y, x, z_hi).
Axes of the slice: x: 4, y: 4, z: 8 (z_hi: 2, z_lo: 4; z = z_hi * 4 + z_lo), core: 2. Of those that a mesh axis runs over, the one named last changes fastest.
Arguments:
- queries: bfloat16 [20480, 768], P(('pb', 'pa')), may hold values from -8 to 8
- passages: bfloat16 [20480, 768], P(('pb', 'pa')), may hold values from -8 to 8
- positives: int32 [20480], P('pb'), may hold values from 0 to 20479, each once
- inv_temp: float32 [], replicated, may hold values from 80 to 320
Outputs:
- query_loss: float32 [20480], P(('pb', 'pa'))
- query_grads: bfloat16 [20480, 768], P(('pb', 'pa'))
- passage_grads: bfloat16 [20480, 768], P(('pb', 'pa'))
The draws below stay inside these ranges and needn't reach their ends.
Inputs may be any that keep to these rules, and one draw needn't show every extreme that they name: `positives`: each passage is the positive of exactly one query.
All inputs are finite; a program needn't handle non-finite values.
Results may differ from the reference program's by a relative error of at most 0.02.
Values may be sent and summed in bfloat16 or wider, within the bound.
No kernel may reach another device: no remote copies, remote signals or barrier semaphores. Data moves between devices by JAX's collectives and lax.ppermute only.
A program may use at most 64 MiB of HBM per device.

```python
import math
import jax
import jax.numpy as jnp
from jax import lax

D = 768
PAIRS = 20480


def draw_queries(key, part):
    key = jax.random.fold_in(key, 11)
    first = jax.random.fold_in(key, 0)
    values = jax.random.normal(first, (PAIRS, D), jnp.float32)
    return jnp.clip(values, -8.0, 8.0).astype(jnp.bfloat16)


def draw_passages(key, part):
    key = jax.random.fold_in(key, 23)
    first = jax.random.fold_in(key, 0)
    values = jax.random.normal(first, (PAIRS, D), jnp.float32)
    return jnp.clip(values, -8.0, 8.0).astype(jnp.bfloat16)


def draw_inv_temp(key, part):
    key = jax.random.fold_in(key, 37)
    return jax.random.uniform(key, (), jnp.float32, 80.0, 120.0)


def setup_inputs(seed: int = 0) -> dict:
    key_of = jax.random.split(jax.random.key(seed), 5)
    queries = draw_queries(jax.random.fold_in(key_of[4], 71), 0)
    passages = draw_passages(jax.random.fold_in(key_of[4], 71), 0)
    positives = jax.random.permutation(key_of[2], PAIRS).astype(jnp.int32)
    inv_temp = draw_inv_temp(jax.random.fold_in(key_of[4], 71), 0)
    return dict(queries=queries, passages=passages, positives=positives, inv_temp=inv_temp)


def unit_rows(values):
    wide = values.astype(jnp.float32)
    length = jnp.sqrt(lax.optimization_barrier(jnp.sum(wide * wide, axis=1, keepdims=True)))
    return (wide / length, length)

def unit_back(unit, length, grad):
    along = lax.optimization_barrier(jnp.sum(unit * grad, axis=1, keepdims=True))
    return ((grad - unit * along) / length).astype(jnp.bfloat16)

def reference(queries, passages, positives, inv_temp):
    query_unit, query_len = unit_rows(queries)
    passage_unit, passage_len = unit_rows(passages)
    query_low = query_unit.astype(jnp.bfloat16)
    passage_low = passage_unit.astype(jnp.bfloat16)
    block = math.gcd(PAIRS, 1024)
    count_blocks = PAIRS // block
    columns = jnp.arange(PAIRS, dtype=jnp.int32)

    def step(carry, inputs):
        rows, targets = inputs
        logits = jnp.dot(rows, passage_low.T, preferred_element_type=jnp.float32) * inv_temp
        total = jax.nn.logsumexp(logits, axis=1)
        hit = columns[None, :] == targets[:, None]
        positive = lax.optimization_barrier(jnp.sum(jnp.where(hit, logits, 0.0), axis=1))
        delta = (jnp.exp(logits - total[:, None]) - jnp.where(hit, 1.0, 0.0)).astype(jnp.bfloat16)
        grad_rows = inv_temp * jnp.dot(delta, passage_low, preferred_element_type=jnp.float32)
        carry = carry + inv_temp * jnp.dot(delta.T, rows, preferred_element_type=jnp.float32)
        return (carry, (total - positive, grad_rows))
    start_grad = jnp.zeros((PAIRS, D), jnp.float32)
    stacked = (query_low.reshape(count_blocks, block, D), positives.reshape(count_blocks, block))
    unit_pgrad, (losses, unit_qgrad) = lax.scan(step, start_grad, stacked)
    query_loss = losses.reshape(PAIRS)
    unit_qgrad = unit_qgrad.reshape(PAIRS, D)
    return (query_loss, unit_back(query_unit, query_len, unit_qgrad), unit_back(passage_unit, passage_len, unit_pgrad))
```

```python
import functools

import jax
import jax.numpy as jnp
from jax import lax
from jax.experimental import pallas as pl
from jax.experimental.pallas import tpu as pltpu
from jax.sharding import Mesh
from jax.sharding import PartitionSpec as P

AXES = ("zl", "core", "y", "x", "zh")
SIZES = (4, 2, 4, 4, 2)
VMEM_LIMIT = 50 * 2**20
F32 = jnp.float32
BF16 = jnp.bfloat16


def device_at(z, core, y, x):
    z, y, x = z % 8, y % 4, x % 4
    return ((((z % 4) * 2 + core) * 4 + y) * 4 + x) * 2 + z // 4


def fetch(array, source):
    pairs = []
    for z in range(8):
        for core in range(2):
            for y in range(4):
                for x in range(4):
                    pairs.append((device_at(*source(z, core, y, x)), device_at(z, core, y, x)))
    return lax.ppermute(array, AXES, pairs)


def swap(array):
    return fetch(array, lambda z, c, y, x: (z, 1 - c, y, x))


def along_z(array, k):
    return fetch(array, lambda z, c, y, x: (z + (k if c == 0 else -k), c, y, x))


def inner(array, k):
    return fetch(array, lambda z, c, y, x: (z, c, y, x + k) if c == 0 else (z, c, y + k, x))


def outer(array, k):
    return fetch(array, lambda z, c, y, x: (z, c, y + k, x) if c == 0 else (z, c, y, x + k))


def norm_kernel(q_ref, p_ref, q_low, p_low):
    for src, dst in ((q_ref, q_low), (p_ref, p_low)):
        wide = src[...].astype(F32)
        length = jnp.sqrt(jnp.sum(wide * wide, axis=1, keepdims=True))
        dst[...] = (wide / length).astype(BF16)


def stats_kernel(rows, tile, offs, temp, target, *refs):
    q_parts, p_parts = refs[:4], refs[4:13]
    e_out, stat, pos_out, q_all, p_all, logits, sems = refs[13:]
    count = rows * 16
    copies = []
    for k, part in enumerate(q_parts):
        for b in range(4):
            copies.append(
                pltpu.make_async_copy(
                    part.at[pl.ds(b * rows, rows)],
                    q_all.at[pl.ds(pl.multiple_of(offs[4 * k + b], 16), rows)],
                    sems.at[len(copies)],
                )
            )
    at = 0
    for part in p_parts:
        size = part.shape[0]
        copies.append(
            pltpu.make_async_copy(part, p_all.at[pl.ds(at, size)], sems.at[len(copies)])
        )
        at += size
    for copy in copies:
        copy.start()
    for copy in copies:
        copy.wait()
    scale = temp[0]
    for t in range(count // tile):
        cols = slice(t * tile, (t + 1) * tile)
        logits[...] = scale * lax.dot_general(
            p_all[...], q_all[cols, :], (((1,), (1,)), ((), ())), preferred_element_type=F32
        )
        values = logits[...]
        top = jnp.max(values, axis=0, keepdims=True)
        hit = lax.broadcasted_iota(jnp.int32, values.shape, 0) == target[:, cols]
        positive = jnp.sum(jnp.where(hit, values, 0.0), axis=0, keepdims=True)
        e = jnp.exp(values - top)
        e_out[:, cols] = e.astype(BF16)
        total = jnp.sum(e, axis=0, keepdims=True)
        stat[:, cols] = jnp.broadcast_to(top, (16, tile))
        stat[:, t * tile + count : (t + 1) * tile + count] = jnp.broadcast_to(total, (16, tile))
        pos_out[:, cols] = positive
    for j in range(16):
        stat[j : j + 1, 2 * count : 2 * count + rows] = pos_out[:, j * rows : (j + 1) * rows]


def grads_kernel(rows, tile, offs, temp, target, own, pos, stat, e_in, q_all, p_all, *refs):
    q_outs, p_outs = refs[:4], refs[4:13]
    total_out, pos_sum, delta, q_grad, p_grad = refs[13:]
    count = rows * 16
    scale = temp[0]
    tops = stat[:, :count]
    top = jnp.max(tops, axis=0, keepdims=True)
    total = top + jnp.log(
        jnp.sum(stat[:, count : 2 * count] * jnp.exp(tops - top), axis=0, keepdims=True)
    )
    total_out[...] = total
    pos_sum[...] = jnp.sum(stat[:, 2 * count :], axis=0, keepdims=True)
    factor = jnp.exp(own[0:1, :count] - total)
    at_hit = jnp.exp(pos[...] - total) - 1.0
    for t in range(count // tile):
        cols = slice(t * tile, (t + 1) * tile)
        hit = lax.broadcasted_iota(jnp.int32, (count, tile), 0) == target[:, cols]
        prob = e_in[:, cols].astype(F32) * factor[:, cols]
        delta[:, cols] = jnp.where(hit, at_hit[:, cols], prob).astype(BF16)
    for t in range(count // tile):
        part = slice(t * tile, (t + 1) * tile)
        p_grad[part, :] = (
            scale * jnp.dot(delta[part, :], q_all[...], preferred_element_type=F32)
        ).astype(BF16)
    at = 0
    for out in p_outs:
        size = out.shape[0]
        out[...] = p_grad[at : at + size, :]
        at += size
    for t in range(count // tile):
        part = slice(t * tile, (t + 1) * tile)
        q_grad[part, :] = (
            scale
            * lax.dot_general(
                delta[:, part], p_all[...], (((0,), (0,)), ((), ())), preferred_element_type=F32
            )
        ).astype(BF16)
    for k, out in enumerate(q_outs):
        for b in range(4):
            out[b * rows : (b + 1) * rows, :] = q_grad[
                pl.ds(pl.multiple_of(offs[4 * k + b], 16), rows), :
            ]


def add_kernel(*refs):
    out = refs[-1]
    total = refs[0][...].astype(F32)
    for ref in refs[1:-1]:
        total = total + ref[...].astype(F32)
    out[...] = total.astype(out.dtype)


def final_kernel(q_ref, p_ref, q0, q1, q2, q3, p0, p1, q_out, p_out):
    def back(src, grad, dst):
        wide = src[...].astype(F32)
        length = jnp.sqrt(jnp.sum(wide * wide, axis=1, keepdims=True))
        unit = wide / length
        along = jnp.sum(unit * grad, axis=1, keepdims=True)
        dst[...] = ((grad - unit * along) / length).astype(BF16)

    q_sum = q0[...].astype(F32) + q1[...].astype(F32) + q2[...].astype(F32) + q3[...].astype(F32)
    back(q_ref, q_sum, q_out)
    back(p_ref, p0[...].astype(F32) + p1[...].astype(F32), p_out)


def vmem(n):
    return [pl.BlockSpec(memory_space=pltpu.VMEM)] * n


def smem(n):
    return [pl.BlockSpec(memory_space=pltpu.SMEM)] * n


def call(kernel, shapes, in_specs, args, scratch=()):
    multi = isinstance(shapes, (list, tuple))
    return pl.pallas_call(
        kernel,
        out_shape=shapes,
        in_specs=in_specs,
        out_specs=vmem(len(shapes)) if multi else vmem(1)[0],
        scratch_shapes=list(scratch),
        compiler_params=pltpu.CompilerParams(vmem_limit_bytes=VMEM_LIMIT),
    )(*args)


def gather_queries(low):
    near = jnp.concatenate([low] + [inner(low, k) for k in (1, 2, 3)], axis=0)
    return [near] + [outer(near, k) for k in (1, 2, 3)]


def gather_passages(low):
    pair = jnp.concatenate([low, swap(low)], axis=0)
    one = along_z(pair, 1)
    two = along_z(pair, 2)
    three = along_z(two, 1)
    four = along_z(two[: low.shape[0]], 2)
    return [pair, one, two, three, four, swap(four), swap(one), swap(two), swap(three)]


def add(shape, dtype, *terms):
    return call(
        add_kernel, jax.ShapeDtypeStruct(shape, dtype), vmem(len(terms)), terms
    )


def scatter_queries(parts, rows):
    terms = [parts[0]] + [outer(parts[k], -k) for k in (1, 2, 3)]
    near = add(parts[0].shape, BF16, *terms)
    return [near[:rows]] + [inner(near[k * rows : (k + 1) * rows], -k) for k in (1, 2, 3)]


def scatter_passages(parts, rows):
    pair, one, two, three, four = parts[:5]
    four_b, one_b, two_b, three_b = (swap(part) for part in parts[5:])
    shape = pair.shape
    three = add(shape, BF16, three, three_b)
    four = add(four.shape, BF16, four, four_b)
    from_three = along_z(three, -1)
    from_four = along_z(four, -2)
    one = add(shape, BF16, one, one_b)
    from_one = along_z(one, -1)
    zero = jnp.zeros_like(from_four)
    two = add(shape, BF16, two, two_b, from_three, jnp.concatenate([from_four, zero], axis=0))
    from_two = along_z(two, -2)
    here = add(shape, BF16, pair, from_one, from_two)
    return here[:rows], swap(here[rows:])


def local(queries, passages, positives, inv_temp):
    rows, width = queries.shape
    count = rows * 16
    tile = 256
    zl, core, y, x, zh = (lax.axis_index(name) for name in AXES)
    z = zh * 4 + zl
    shape = jax.ShapeDtypeStruct
    q_low, p_low = call(
        norm_kernel, [shape((rows, width), BF16)] * 2, vmem(2), (queries, passages)
    )
    q_parts = gather_queries(q_low)
    p_parts = gather_passages(p_low)

    near, far = jnp.arange(16) % 4, jnp.arange(16) // 4
    from_y = (y + jnp.where(core == 0, far, near)) % 4
    from_x = (x + jnp.where(core == 0, near, far)) % 4
    offs = ((from_y * 4 + from_x) * rows).astype(jnp.int32)

    wanted = lax.dynamic_index_in_dim(positives.reshape(16, 2, rows), zh, 1, keepdims=False)
    block = wanted // rows
    owner_z = (block % 2) * 4 + block // 64
    owner_core = (block // 32) % 2
    other = (owner_core != core).astype(jnp.int32)
    away = jnp.where(core == 0, owner_z - z, z - owner_z) % 8
    slot = jnp.where(
        away < 4,
        2 * away + other,
        jnp.where(away == 4, 8 + other, 10 + 2 * (7 - away) + 1 - other),
    )
    present = (block // 8) % 4 * 4 + (block // 2) % 4 == y * 4 + x
    target = jnp.where(present, slot * rows + wanted % rows, -1).reshape(1, count)
    temp = inv_temp.reshape(1)

    stat_width = 2 * count + -(-rows // 128) * 128
    e, stat, pos, q_all, p_all = call(
        functools.partial(stats_kernel, rows, tile),
        [
            shape((count, count), BF16),
            shape((16, stat_width), F32),
            shape((1, count), F32),
            shape((count, width), BF16),
            shape((count, width), BF16),
        ],
        smem(2) + vmem(1) + [pl.BlockSpec(memory_space=pl.ANY)] * 13,
        (offs, temp, target, *q_parts, *p_parts),
        [pltpu.VMEM((count, tile), F32), pltpu.SemaphoreType.DMA((25,))],
    )
    stats = lax.all_to_all(stat, ("y", "x"), 0, 0, tiled=True)

    grads = call(
        functools.partial(grads_kernel, rows, tile),
        [shape(part.shape, BF16) for part in (*q_parts, *p_parts)]
        + [shape((1, count), F32), shape((1, stat_width - 2 * count), F32)],
        smem(2) + vmem(7),
        (offs, temp, target, stat, pos, stats, e, q_all, p_all),
        [
            pltpu.VMEM((count, count), BF16),
            pltpu.VMEM((count, width), BF16),
            pltpu.VMEM((count, width), BF16),
        ],
    )
    q_terms = scatter_queries(grads[:4], rows)
    p_terms = scatter_passages(grads[4:13], rows)
    total, pos_sum = grads[13:]
    mine = lax.dynamic_slice_in_dim(total[0], (y * 4 + x) * rows, rows, 0)
    query_loss = mine - pos_sum[0, :rows]
    query_grads, passage_grads = call(
        final_kernel,
        [shape((rows, width), BF16)] * 2,
        vmem(8),
        (queries, passages, *q_terms, *p_terms),
    )
    return (query_loss, query_grads, passage_grads)


def solution(mesh):
    fine = Mesh(mesh.devices.reshape(SIZES), AXES)
    return jax.shard_map(
        local,
        mesh=fine,
        in_specs=(P(AXES, None), P(AXES, None), P(("zl", "core")), P()),
        out_specs=(P(AXES), P(AXES, None), P(AXES, None)),
        check_vma=False,
    )
```

```python
import functools

import jax
import jax.numpy as jnp
from jax import lax
from jax.experimental import pallas as pl
from jax.experimental.pallas import tpu as pltpu
from jax.sharding import Mesh
from jax.sharding import PartitionSpec as P

AXES = ("zl", "core", "y", "x", "zh")
SIZES = (4, 2, 4, 4, 2)
VMEM_LIMIT = 24 * 2**20
F32 = jnp.float32
BF16 = jnp.bfloat16


def device_at(z, core, y, x):
    z, y, x = z % 8, y % 4, x % 4
    return ((((z % 4) * 2 + core) * 4 + y) * 4 + x) * 2 + z // 4


def fetch(array, source):
    pairs = []
    for z in range(8):
        for core in range(2):
            for y in range(4):
                for x in range(4):
                    pairs.append((device_at(*source(z, core, y, x)), device_at(z, core, y, x)))
    return lax.ppermute(array, AXES, pairs)


def swap(array):
    return fetch(array, lambda z, c, y, x: (z, 1 - c, y, x))


def along_z(array, k):
    return fetch(array, lambda z, c, y, x: (z + (k if c == 0 else -k), c, y, x))


def inner(array, k):
    return fetch(array, lambda z, c, y, x: (z, c, y, x + k) if c == 0 else (z, c, y + k, x))


def outer(array, k):
    return fetch(array, lambda z, c, y, x: (z, c, y + k, x) if c == 0 else (z, c, y, x + k))


def norm_kernel(q_ref, p_ref, q_low, p_low):
    for src, dst in ((q_ref, q_low), (p_ref, p_low)):
        wide = src[...].astype(F32)
        length = jnp.sqrt(jnp.sum(wide * wide, axis=1, keepdims=True))
        dst[...] = (wide / length).astype(BF16)


def logits_kernel(chunk, temp, *refs):
    parts = (len(refs) - 2) // 4
    q_parts, targets, p_all = refs[:parts], refs[parts : 2 * parts], refs[2 * parts]
    e_outs, row_outs = refs[2 * parts + 1 : 3 * parts + 1], refs[3 * parts + 1 : 4 * parts + 1]
    logits = refs[-1]
    count = p_all.shape[0]
    scale = temp[0]
    for q, target, e_out, row_out in zip(q_parts, targets, e_outs, row_outs):
        tops = []
        for at in range(0, count, chunk):
            part = slice(at, at + chunk)
            values = scale * lax.dot_general(
                p_all[part, :], q[...], (((1,), (1,)), ((), ())), preferred_element_type=F32
            )
            logits[part, :] = values
            tops.append(jnp.max(values, axis=0, keepdims=True))
        top = functools.reduce(jnp.maximum, tops)
        total = jnp.zeros_like(top)
        positive = jnp.zeros_like(top)
        for at in range(0, count, chunk):
            part = slice(at, at + chunk)
            values = logits[part, :]
            hit = lax.broadcasted_iota(jnp.int32, values.shape, 0) + at == target[...]
            positive = positive + jnp.sum(jnp.where(hit, values, 0.0), axis=0, keepdims=True)
            e = jnp.exp(values - top)
            total = total + jnp.sum(e, axis=0, keepdims=True)
            e_out[part, :] = e.astype(BF16)
        row_out[0:1, :] = top
        row_out[1:2, :] = top + jnp.log(total)
        row_out[2:3, :] = positive


def join_kernel(*refs):
    out = refs[-1]
    at = 0
    for part in refs[:-1]:
        out[at : at + part.shape[0], :] = part[...]
        at += part.shape[0]


def stat_kernel(rows, slots, *refs):
    stat = refs[-1]
    stat[...] = jnp.zeros_like(stat)
    positive = jnp.zeros((16, rows), F32)
    dest = lax.broadcasted_iota(jnp.int32, (16, rows), 0)
    for k, part in enumerate(refs[:-1]):
        for b in range(4):
            slot = slots[4 * k + b]
            lanes = slice(b * rows, (b + 1) * rows)
            stat[:, pl.ds(pl.multiple_of(slot * 128, 128), rows)] = jnp.broadcast_to(
                part[1:2, lanes], (16, rows)
            )
            positive = jnp.where(dest == slot, part[2:3, lanes], positive)
    stat[:, 2048 : 2048 + rows] = positive


def p_grads_kernel(rows, chunk, first, slots, temp, stat, *refs):
    e_parts, row_parts, targets, q_parts = refs[:4], refs[4:8], refs[8:12], refs[12:16]
    delta, q_all, total_out, pos_sum, grad, lane = refs[16:]
    count = delta.shape[0]
    width = e_parts[0].shape[1]
    scale = temp[0]
    sums = stat[:, :2048]
    top = jnp.max(sums, axis=0, keepdims=True)
    total_out[...] = top + jnp.log(jnp.sum(jnp.exp(sums - top), axis=0, keepdims=True))
    pos_sum[...] = jnp.sum(stat[:, 2048:], axis=0, keepdims=True)
    for k in range(4):
        q_all[k * width : (k + 1) * width, :] = q_parts[k][...]
        for b in range(4):
            lane[0:1, b * rows : (b + 1) * rows] = total_out[
                :, pl.ds(pl.multiple_of(slots[4 * k + b] * 128, 128), rows)
            ]
        total = lane[0:1, :]
        factor = jnp.exp(row_parts[k][0:1, :] - total)
        at_hit = jnp.exp(row_parts[k][2:3, :] - total) - 1.0
        for at in range(0, count, chunk):
            part = slice(at, at + chunk)
            prob = e_parts[k][part, :].astype(F32) * factor
            hit = lax.broadcasted_iota(jnp.int32, prob.shape, 0) + at == targets[k][...]
            delta[part, k * width : (k + 1) * width] = jnp.where(hit, at_hit, prob).astype(BF16)
    for at in range(first, count, chunk):
        size = min(chunk, count - at)
        grad[at - first : at - first + size, :] = (
            scale * jnp.dot(delta[at : at + size, :], q_all[...], preferred_element_type=F32)
        ).astype(BF16)


def p_rest_kernel(chunk, temp, delta, q_all, grad):
    scale = temp[0]
    count = grad.shape[0]
    for at in range(0, count, chunk):
        size = min(chunk, count - at)
        grad[at : at + size, :] = (
            scale * jnp.dot(delta[at : at + size, :], q_all[...], preferred_element_type=F32)
        ).astype(BF16)


def q_grads_kernel(temp, delta, p_all, *outs):
    scale = temp[0]
    width = outs[0].shape[0]
    for k, out in enumerate(outs):
        out[...] = (
            scale
            * lax.dot_general(
                delta[:, k * width : (k + 1) * width],
                p_all[...],
                (((0,), (0,)), ((), ())),
                preferred_element_type=F32,
            )
        ).astype(BF16)


def add_kernel(*refs):
    out = refs[-1]
    total = refs[0][...].astype(F32)
    for ref in refs[1:-1]:
        total = total + ref[...].astype(F32)
    out[...] = total.astype(out.dtype)


def final_kernel(q_ref, p_ref, q0, q1, q2, q3, p0, p1, q_out, p_out):
    def back(src, grad, dst):
        wide = src[...].astype(F32)
        length = jnp.sqrt(jnp.sum(wide * wide, axis=1, keepdims=True))
        unit = wide / length
        along = jnp.sum(unit * grad, axis=1, keepdims=True)
        dst[...] = ((grad - unit * along) / length).astype(BF16)

    q_sum = q0[...].astype(F32) + q1[...].astype(F32) + q2[...].astype(F32) + q3[...].astype(F32)
    back(q_ref, q_sum, q_out)
    back(p_ref, p0[...].astype(F32) + p1[...].astype(F32), p_out)


def vmem(n):
    return [pl.BlockSpec(memory_space=pltpu.VMEM)] * n


def smem(n):
    return [pl.BlockSpec(memory_space=pltpu.SMEM)] * n


def call(kernel, shapes, in_specs, args, scratch=()):
    multi = isinstance(shapes, (list, tuple))
    return pl.pallas_call(
        kernel,
        out_shape=shapes,
        in_specs=in_specs,
        out_specs=vmem(len(shapes)) if multi else vmem(1)[0],
        scratch_shapes=list(scratch),
        compiler_params=pltpu.CompilerParams(vmem_limit_bytes=VMEM_LIMIT),
    )(*args)


def gather_queries(low):
    near = jnp.concatenate([low] + [inner(low, k) for k in (1, 2, 3)], axis=0)
    return [near] + [outer(near, k) for k in (1, 2, 3)]


def gather_passages(low, after):
    pair = jnp.concatenate([low, swap(low)], axis=0)
    one = along_z(pair, 1)
    two = along_z(pair, 2)
    two, one, _ = lax.optimization_barrier((two, one, after))
    three = along_z(two, 1)
    four = along_z(two[: low.shape[0]], 2)
    return [pair, one, two, three, four, swap(four), swap(one), swap(two), swap(three)]


def add(shape, dtype, *terms):
    return call(
        add_kernel, jax.ShapeDtypeStruct(shape, dtype), vmem(len(terms)), terms
    )


def scatter_queries(parts, rows):
    terms = [parts[0]] + [outer(parts[k], -k) for k in (1, 2, 3)]
    near = add(parts[0].shape, BF16, *terms)
    return [near[:rows]] + [inner(near[k * rows : (k + 1) * rows], -k) for k in (1, 2, 3)]


def scatter_passages(first, last, rows):
    pair, one, two = (first[2 * k * rows : 2 * (k + 1) * rows] for k in range(3))
    three, four, rest = last[: 2 * rows], last[2 * rows : 3 * rows], last[3 * rows :]
    crossed = swap(rest)
    four_b = crossed[:rows]
    one_b, two_b, three_b = (crossed[(2 * k + 1) * rows : (2 * k + 3) * rows] for k in range(3))
    shape = pair.shape
    three = add(shape, BF16, three, three_b)
    four = add(four.shape, BF16, four, four_b)
    from_three = along_z(three, -1)
    from_four = along_z(four, -2)
    one = add(shape, BF16, one, one_b)
    from_one = along_z(one, -1)
    zero = jnp.zeros_like(from_four)
    two = add(shape, BF16, two, two_b, from_three, jnp.concatenate([from_four, zero], axis=0))
    from_two = along_z(two, -2)
    here = add(shape, BF16, pair, from_one, from_two)
    return here[:rows], swap(here[rows:])


def local(queries, passages, positives, inv_temp):
    rows, width = queries.shape
    count = rows * 16
    zl, core, y, x, zh = (lax.axis_index(name) for name in AXES)
    z = zh * 4 + zl
    shape = jax.ShapeDtypeStruct
    q_low, p_low = call(
        norm_kernel, [shape((rows, width), BF16)] * 2, vmem(2), (queries, passages)
    )
    q_parts = gather_queries(q_low)
    p_parts = gather_passages(p_low, q_parts[0])

    near, far = jnp.arange(16) % 4, jnp.arange(16) // 4
    from_y = (y + jnp.where(core == 0, far, near)) % 4
    from_x = (x + jnp.where(core == 0, near, far)) % 4
    slots = (from_y * 4 + from_x).astype(jnp.int32)

    wanted = lax.dynamic_index_in_dim(positives.reshape(16, 2, rows), zh, 1, keepdims=False)
    wanted = wanted[slots]
    block = wanted // rows
    owner_z = (block % 2) * 4 + block // 64
    owner_core = (block // 32) % 2
    other = (owner_core != core).astype(jnp.int32)
    away = jnp.where(core == 0, owner_z - z, z - owner_z) % 8
    slot = jnp.where(
        away < 4,
        2 * away + other,
        jnp.where(away == 4, 8 + other, 10 + 2 * (7 - away) + 1 - other),
    )
    present = (block // 8) % 4 * 4 + (block // 2) % 4 == y * 4 + x
    target = jnp.where(present, slot * rows + wanted % rows, -1).reshape(4, 1, 4 * rows)
    targets = [target[k] for k in range(4)]
    temp = inv_temp.reshape(1)
    chunk = 256
    part_rows = 4 * rows

    p_all = call(join_kernel, shape((count, width), BF16), vmem(9), p_parts)

    def logits(*ks):
        out = call(
            functools.partial(logits_kernel, chunk),
            [shape((count, part_rows), BF16)] * len(ks) + [shape((8, part_rows), F32)] * len(ks),
            smem(1) + vmem(2 * len(ks) + 1),
            (temp, *(q_parts[k] for k in ks), *(targets[k] for k in ks), p_all),
            [pltpu.VMEM((count, part_rows), F32)],
        )
        return dict(zip(ks, zip(out[: len(ks)], out[len(ks) :])))

    found = {**logits(0), **logits(1, 3), **logits(2)}
    e_parts = [found[k][0] for k in range(4)]
    row_parts = [found[k][1] for k in range(4)]
    stat = call(
        functools.partial(stat_kernel, rows),
        shape((16, 17 * 128), F32),
        smem(1) + vmem(4),
        (slots, *row_parts),
    )
    stats = lax.all_to_all(stat, ("y", "x"), 0, 0, tiled=True)

    first = 6 * rows
    delta, q_all, total, pos_sum, p_last = call(
        functools.partial(p_grads_kernel, rows, chunk, first),
        [
            shape((count, count), BF16),
            shape((count, width), BF16),
            shape((1, 16 * 128), F32),
            shape((1, 128), F32),
            shape((count - first, width), BF16),
        ],
        smem(2) + vmem(17),
        (slots, temp, stats, *e_parts, *row_parts, *targets, *q_parts),
        [pltpu.VMEM((8, part_rows), F32)],
    )
    p_first = call(
        functools.partial(p_rest_kernel, chunk),
        shape((first, width), BF16),
        smem(1) + vmem(2),
        (temp, delta, q_all),
    )
    q_grads = call(
        q_grads_kernel,
        [shape((part_rows, width), BF16)] * 4,
        smem(1) + vmem(2),
        (temp, delta, p_all),
    )
    q_terms = scatter_queries(q_grads, rows)
    p_terms = scatter_passages(p_first, p_last, rows)
    mine = lax.dynamic_slice_in_dim(total[0], (y * 4 + x) * 128, rows, 0)
    query_loss = mine - pos_sum[0, :rows]
    query_grads, passage_grads = call(
        final_kernel,
        [shape((rows, width), BF16)] * 2,
        vmem(8),
        (queries, passages, *q_terms, *p_terms),
    )
    return (query_loss, query_grads, passage_grads)


def solution(mesh):
    fine = Mesh(mesh.devices.reshape(SIZES), AXES)
    return jax.shard_map(
        local,
        mesh=fine,
        in_specs=(P(AXES, None), P(AXES, None), P(("zl", "core")), P()),
        out_specs=(P(AXES), P(AXES, None), P(AXES, None)),
        check_vma=False,
    )
```

```python
import functools

import jax
import jax.numpy as jnp
from jax import lax
from jax.experimental import pallas as pl
from jax.experimental.pallas import tpu as pltpu
from jax.sharding import Mesh
from jax.sharding import PartitionSpec as P

AXES = ("zl", "core", "y", "x", "zh")
SIZES = (4, 2, 4, 4, 2)
VMEM_LIMIT = 24 * 2**20
F32 = jnp.float32
BF16 = jnp.bfloat16


def device_at(z, core, y, x):
    z, y, x = z % 8, y % 4, x % 4
    return ((((z % 4) * 2 + core) * 4 + y) * 4 + x) * 2 + z // 4


def fetch(array, source):
    pairs = []
    for z in range(8):
        for core in range(2):
            for y in range(4):
                for x in range(4):
                    pairs.append((device_at(*source(z, core, y, x)), device_at(z, core, y, x)))
    return lax.ppermute(array, AXES, pairs)


def swap(array):
    return fetch(array, lambda z, c, y, x: (z, 1 - c, y, x))


def along_z(array, k):
    return fetch(array, lambda z, c, y, x: (z + (k if c == 0 else -k), c, y, x))


def inner(array, k):
    return fetch(array, lambda z, c, y, x: (z, c, y, x + k) if c == 0 else (z, c, y + k, x))


def outer(array, k):
    return fetch(array, lambda z, c, y, x: (z, c, y + k, x) if c == 0 else (z, c, y, x + k))


def place():
    return tuple(lax.axis_index(name) for name in AXES)


def slot_of(k, b):
    _, core, y, x, _ = place()
    step_y = jnp.where(core == 0, k, b)
    step_x = jnp.where(core == 0, b, k)
    return lax.rem(y + step_y, 4) * 4 + lax.rem(x + step_x, 4)


def norm_kernel(q_ref, p_ref, q_low, p_low, q_buf, p_buf, sems):
    copies = [
        pltpu.make_async_copy(src, buf, sems.at[i])
        for i, (src, buf) in enumerate(((q_ref, q_buf), (p_ref, p_buf)))
    ]
    for copy in copies:
        copy.start()
    for copy, buf, dst in zip(copies, (q_buf, p_buf), (q_low, p_low)):
        copy.wait()
        wide = buf[...].astype(F32)
        length = jnp.sqrt(jnp.sum(wide * wide, axis=1, keepdims=True))
        dst[...] = (wide / length).astype(BF16)


def target_kernel(rows, positives, *outs):
    zl, core, y, x, zh = place()
    z = zh * 4 + zl
    for k, out in enumerate(outs):
        for b in range(4):
            wanted = positives[pl.ds(slot_of(k, b) * 2 + zh, 1), :]
            block = lax.div(wanted, rows)
            owner_z = lax.rem(block, 2) * 4 + lax.div(block, 64)
            other = (lax.rem(lax.div(block, 32), 2) != core).astype(jnp.int32)
            away = lax.rem(jnp.where(core == 0, owner_z - z, z - owner_z) + 8, 8)
            slot = jnp.where(
                away < 4,
                2 * away + other,
                jnp.where(away == 4, 8 + other, 10 + 2 * (7 - away) + 1 - other),
            )
            owner = lax.rem(lax.div(block, 8), 4) * 4 + lax.rem(lax.div(block, 2), 4)
            row = slot * rows + lax.rem(wanted, rows)
            out[:, b * rows : (b + 1) * rows] = jnp.where(owner == y * 4 + x, row, -1)


def logits_kernel(chunk, temp, *refs):
    parts = (len(refs) - 2) // 4
    q_parts, targets, p_all = refs[:parts], refs[parts : 2 * parts], refs[2 * parts]
    e_outs, row_outs = refs[2 * parts + 1 : 3 * parts + 1], refs[3 * parts + 1 : 4 * parts + 1]
    logits = refs[-1]
    count = p_all.shape[0]
    scale = temp[0]
    for q, target, e_out, row_out in zip(q_parts, targets, e_outs, row_outs):
        tops = []
        for at in range(0, count, chunk):
            part = slice(at, at + chunk)
            values = scale * lax.dot_general(
                p_all[part, :], q[...], (((1,), (1,)), ((), ())), preferred_element_type=F32
            )
            logits[part, :] = values
            tops.append(jnp.max(values, axis=0, keepdims=True))
        top = functools.reduce(jnp.maximum, tops)
        total = jnp.zeros_like(top)
        positive = jnp.zeros_like(top)
        for at in range(0, count, chunk):
            part = slice(at, at + chunk)
            values = logits[part, :]
            hit = lax.broadcasted_iota(jnp.int32, values.shape, 0) + at == target[...]
            positive = positive + jnp.sum(jnp.where(hit, values, 0.0), axis=0, keepdims=True)
            e = jnp.exp(values - top)
            total = total + jnp.sum(e, axis=0, keepdims=True)
            e_out[part, :] = e.astype(BF16)
        row_out[0:1, :] = top
        row_out[1:2, :] = top + jnp.log(total)
        row_out[2:3, :] = positive


def join_kernel(*refs):
    out = refs[-1]
    at = 0
    for part in refs[:-1]:
        size = min(part.shape[0], out.shape[0] - at)
        out[at : at + size, :] = part[:size, :]
        at += size


def stat_kernel(rows, *refs):
    stat = refs[-1]
    stat[...] = jnp.zeros_like(stat)
    positive = jnp.zeros((16, rows), F32)
    dest = lax.broadcasted_iota(jnp.int32, (16, rows), 0)
    for k, part in enumerate(refs[:-1]):
        for b in range(4):
            slot = slot_of(k, b)
            lanes = slice(b * rows, (b + 1) * rows)
            stat[:, pl.ds(pl.multiple_of(slot * 128, 128), rows)] = jnp.broadcast_to(
                part[1:2, lanes], (16, rows)
            )
            positive = jnp.where(dest == slot, part[2:3, lanes], positive)
    stat[:, 2048 : 2048 + rows] = positive


def delta_kernel(rows, chunk, stat, *refs):
    e_parts, row_parts, targets, deltas = refs[:4], refs[4:8], refs[8:12], refs[12:16]
    loss, totals, lane = refs[16:]
    count = e_parts[0].shape[0]
    sums = stat[:, :2048]
    top = jnp.max(sums, axis=0, keepdims=True)
    totals[0:1, :] = top + jnp.log(jnp.sum(jnp.exp(sums - top), axis=0, keepdims=True))
    own = totals[0:1, pl.ds(pl.multiple_of(slot_of(0, 0) * 128, 128), rows)]
    loss[...] = own - jnp.sum(stat[:, 2048:], axis=0, keepdims=True)[:, :rows]
    for k in range(4):
        for b in range(4):
            lane[k : k + 1, b * rows : (b + 1) * rows] = totals[
                0:1, pl.ds(pl.multiple_of(slot_of(k, b) * 128, 128), rows)
            ]
    for k in range(4):
        total = lane[k : k + 1, :]
        factor = jnp.exp(row_parts[k][0:1, :] - total)
        at_hit = jnp.exp(row_parts[k][2:3, :] - total) - 1.0
        for at in range(0, count, chunk):
            part = slice(at, at + chunk)
            prob = e_parts[k][part, :].astype(F32) * factor
            hit = lax.broadcasted_iota(jnp.int32, prob.shape, 0) + at == targets[k][...]
            deltas[k][part, :] = jnp.where(hit, at_hit, prob).astype(BF16)


def p_grads_kernel(first, temp, *refs):
    deltas, q_parts, outs = refs[:4], refs[4:8], refs[8:]
    at = first
    for out in outs:
        size = out.shape[0]
        total = jnp.zeros(out.shape, F32)
        for delta, q in zip(deltas, q_parts):
            total = total + jnp.dot(
                delta[at : at + size, :], q[...], preferred_element_type=F32
            )
        out[...] = (temp[0] * total).astype(BF16)
        at += size


def q_grads_kernel(temp, delta, p_all, out):
    out[...] = (
        temp[0]
        * lax.dot_general(
            delta[...], p_all[...], (((0,), (0,)), ((), ())), preferred_element_type=F32
        )
    ).astype(BF16)


def add_kernel(starts, *refs):
    terms, outs = refs[: len(starts)], refs[len(starts) :]
    at = 0
    for out in outs:
        size = out.shape[0]
        total = None
        for term, start in zip(terms, starts):
            if start + at + size > term.shape[0]:
                continue
            value = term[start + at : start + at + size, :].astype(F32)
            total = value if total is None else total + value
        out[...] = total.astype(out.dtype)
        at += size


def final_kernel(q_ref, p_ref, q0, q1, q2, q3, p0, p1, q_out, p_out):
    def back(src, grad, dst):
        wide = src[...].astype(F32)
        length = jnp.sqrt(jnp.sum(wide * wide, axis=1, keepdims=True))
        unit = wide / length
        along = jnp.sum(unit * grad, axis=1, keepdims=True)
        dst[...] = ((grad - unit * along) / length).astype(BF16)

    q_sum = q0[...].astype(F32) + q1[...].astype(F32) + q2[...].astype(F32) + q3[...].astype(F32)
    back(q_ref, q_sum, q_out)
    back(p_ref, p0[...].astype(F32) + p1[...].astype(F32), p_out)


def vmem(n):
    return [pl.BlockSpec(memory_space=pltpu.VMEM)] * n


def anywhere(n):
    return [pl.BlockSpec(memory_space=pl.ANY)] * n


def smem(n):
    return [pl.BlockSpec(memory_space=pltpu.SMEM)] * n


def call(kernel, shapes, in_specs, args, scratch=()):
    multi = isinstance(shapes, (list, tuple))
    return pl.pallas_call(
        kernel,
        out_shape=shapes,
        in_specs=in_specs,
        out_specs=vmem(len(shapes)) if multi else vmem(1)[0],
        scratch_shapes=list(scratch),
        compiler_params=pltpu.CompilerParams(vmem_limit_bytes=VMEM_LIMIT),
    )(*args)


def join(rows, *parts):
    return call(
        join_kernel,
        jax.ShapeDtypeStruct((rows, parts[0].shape[1]), BF16),
        vmem(len(parts)),
        parts,
    )


def after(array, *others):
    return lax.optimization_barrier((array, *others))[0]


def gather(q_low, p_low):
    rows = q_low.shape[0]
    pair = join(2 * rows, p_low, swap(p_low))
    near = join(4 * rows, q_low, *(inner(q_low, k) for k in (1, 2, 3)))
    one = along_z(pair, 1)
    two = along_z(pair, 2)
    near = after(near, one)
    far = [outer(near, k) for k in (1, 2, 3)]
    relay = after(two, near)
    three = along_z(relay, 1)
    four = along_z(join(rows, relay), 2)
    one_b = swap(after(one, *far))
    two_b = swap(after(two, *far))
    return [near, *far], [pair, one, two, three, four, swap(four), one_b, two_b, swap(three)]


def add(sizes, *terms):
    width = terms[0][0].shape[1]
    return call(
        functools.partial(add_kernel, [start for _, start in terms]),
        [jax.ShapeDtypeStruct((size, width), BF16) for size in sizes],
        vmem(len(terms)),
        [array for array, _ in terms],
    )


def scatter_queries(parts, rows):
    terms = [parts[0]] + [outer(parts[k], -k) for k in (1, 2, 3)]
    near = add([rows] * 4, *((term, 0) for term in terms))
    return [near[0]] + [inner(near[k], -k) for k in (1, 2, 3)]


def scatter_passages(pair, one, two, three, four, rest, rows):
    crossed = swap(rest)
    (three,) = add([2 * rows], (three, 0), (crossed, 5 * rows))
    (four,) = add([rows], (four, 0), (crossed, 0))
    from_three = along_z(three, -1)
    from_four = along_z(four, -2)
    (one,) = add([2 * rows], (one, 0), (crossed, rows))
    from_one = along_z(one, -1)
    two = add([rows] * 2, (two, 0), (crossed, 3 * rows), (from_three, 0), (from_four, 0))
    from_two = along_z(join(2 * rows, *two), -2)
    here, there = add([rows] * 2, (pair, 0), (from_one, 0), (from_two, 0))
    return here, swap(there)


def local(queries, passages, positives, inv_temp):
    rows, width = queries.shape
    count = rows * 16
    part_rows = 4 * rows
    chunk = 256
    shape = jax.ShapeDtypeStruct
    temp = inv_temp.reshape(1)
    q_low, p_low = call(
        norm_kernel,
        [shape((rows, width), BF16)] * 2,
        anywhere(2),
        (queries, passages),
        [pltpu.VMEM((rows, width), BF16)] * 2 + [pltpu.SemaphoreType.DMA((2,))],
    )
    q_parts, p_parts = gather(q_low, p_low)
    targets = call(
        functools.partial(target_kernel, rows),
        [shape((1, part_rows), jnp.int32)] * 4,
        vmem(1),
        (positives.reshape(32, rows),),
    )
    p_all = join(count, *p_parts)

    def logits(*ks):
        out = call(
            functools.partial(logits_kernel, chunk),
            [shape((count, part_rows), BF16)] * len(ks) + [shape((8, part_rows), F32)] * len(ks),
            smem(1) + vmem(2 * len(ks) + 1),
            (temp, *(q_parts[k] for k in ks), *(targets[k] for k in ks), p_all),
            [pltpu.VMEM((count, part_rows), F32)],
        )
        return dict(zip(ks, zip(out[: len(ks)], out[len(ks) :])))

    found = {**logits(0), **logits(1, 3), **logits(2)}
    e_parts = [found[k][0] for k in range(4)]
    row_parts = [found[k][1] for k in range(4)]
    stat = call(
        functools.partial(stat_kernel, rows), shape((16, 17 * 128), F32), vmem(4), row_parts
    )
    stats = lax.all_to_all(stat, ("y", "x"), 0, 0, tiled=True)

    *deltas, loss = call(
        functools.partial(delta_kernel, rows, chunk),
        [shape((count, part_rows), BF16)] * 4 + [shape((1, rows), F32)],
        vmem(13),
        (stats, *e_parts, *row_parts, *targets),
        [pltpu.VMEM((8, 16 * 128), F32), pltpu.VMEM((8, part_rows), F32)],
    )

    def p_grads(first, *sizes):
        return call(
            functools.partial(p_grads_kernel, first * rows),
            [shape((size * rows, width), BF16) for size in sizes],
            smem(1) + vmem(8),
            (temp, *deltas, *q_parts),
        )

    three, four, rest = p_grads(6, 2, 1, 7)
    q_grads = [
        call(q_grads_kernel, shape((part_rows, width), BF16), smem(1) + vmem(2), (temp, delta, p_all))
        for delta in deltas
    ]
    pair, one, two = p_grads(0, 2, 2, 2)
    q_terms = scatter_queries(q_grads, rows)
    p_terms = scatter_passages(pair, one, two, three, four, rest, rows)
    query_grads, passage_grads = call(
        final_kernel,
        [shape((rows, width), BF16)] * 2,
        vmem(8),
        (queries, passages, *q_terms, *p_terms),
    )
    return (loss.reshape(rows), query_grads, passage_grads)


def solution(mesh):
    fine = Mesh(mesh.devices.reshape(SIZES), AXES)
    return jax.shard_map(
        local,
        mesh=fine,
        in_specs=(P(AXES, None), P(AXES, None), P(("zl", "core")), P()),
        out_specs=(P(AXES), P(AXES, None), P(AXES, None)),
        check_vma=False,
    )
```

```python
import functools

import jax
import jax.numpy as jnp
from jax import lax
from jax.experimental import pallas as pl
from jax.experimental.pallas import tpu as pltpu
from jax.sharding import Mesh
from jax.sharding import PartitionSpec as P

AXES = ("zl", "core", "y", "x", "zh")
SIZES = (4, 2, 4, 4, 2)
VMEM_LIMIT = 24 * 2**20
F32 = jnp.float32
BF16 = jnp.bfloat16


def device_at(z, core, y, x):
    z, y, x = z % 8, y % 4, x % 4
    return ((((z % 4) * 2 + core) * 4 + y) * 4 + x) * 2 + z // 4


def fetch(array, source):
    pairs = []
    for z in range(8):
        for core in range(2):
            for y in range(4):
                for x in range(4):
                    pairs.append((device_at(*source(z, core, y, x)), device_at(z, core, y, x)))
    return lax.ppermute(array, AXES, pairs)


def swap(array):
    return fetch(array, lambda z, c, y, x: (z, 1 - c, y, x))


def along_z(array, k):
    return fetch(array, lambda z, c, y, x: (z + (k if c == 0 else -k), c, y, x))


def inner(array, k):
    return fetch(array, lambda z, c, y, x: (z, c, y, x + k) if c == 0 else (z, c, y + k, x))


def outer(array, k):
    return fetch(array, lambda z, c, y, x: (z, c, y + k, x) if c == 0 else (z, c, y, x + k))


def place():
    return tuple(lax.axis_index(name) for name in AXES)


def slot_of(k, b):
    _, core, y, x, _ = place()
    step_y = jnp.where(core == 0, k, b)
    step_x = jnp.where(core == 0, b, k)
    return lax.rem(y + step_y, 4) * 4 + lax.rem(x + step_x, 4)


def norm_kernel(src, dst):
    wide = src[...].astype(F32)
    length = jnp.sqrt(jnp.sum(wide * wide, axis=1, keepdims=True))
    dst[...] = (wide / length).astype(BF16)


def target_kernel(rows, positives, *outs):
    zl, core, y, x, zh = place()
    z = zh * 4 + zl
    for k, out in enumerate(outs):
        for b in range(4):
            wanted = positives[pl.ds(slot_of(k, b) * 2 + zh, 1), :]
            block = lax.div(wanted, rows)
            owner_z = lax.rem(block, 2) * 4 + lax.div(block, 64)
            other = (lax.rem(lax.div(block, 32), 2) != core).astype(jnp.int32)
            away = lax.rem(jnp.where(core == 0, owner_z - z, z - owner_z) + 8, 8)
            slot = jnp.where(
                away < 4,
                2 * away + other,
                jnp.where(away == 4, 8 + other, 10 + 2 * (7 - away) + 1 - other),
            )
            owner = lax.rem(lax.div(block, 8), 4) * 4 + lax.rem(lax.div(block, 2), 4)
            row = slot * rows + lax.rem(wanted, rows)
            out[:, b * rows : (b + 1) * rows] = jnp.where(owner == y * 4 + x, row, -1)


def logits_kernel(rows, chunk, temp, *refs):
    q_parts, targets, p_parts = refs[:4], refs[4:8], refs[8:17]
    p_all, stat, e_outs, row_outs, logits = refs[17], refs[18], refs[19:23], refs[23:27], refs[27]
    count = p_all.shape[0]
    scale = temp[0]
    at = 0
    for part in p_parts:
        p_all[at : at + part.shape[0], :] = part[...]
        at += part.shape[0]
    stat[...] = jnp.zeros_like(stat)
    dest = lax.broadcasted_iota(jnp.int32, (16, rows), 0)
    for_dest = jnp.zeros((16, rows), F32)
    for k in range(4):
        tops = []
        for at in range(0, count, chunk):
            part = slice(at, at + chunk)
            values = scale * lax.dot_general(
                p_all[part, :], q_parts[k][...], (((1,), (1,)), ((), ())), preferred_element_type=F32
            )
            logits[k % 2, part, :] = values
            tops.append(jnp.max(values, axis=0, keepdims=True))
        top = functools.reduce(jnp.maximum, tops)
        total = jnp.zeros_like(top)
        positive = jnp.zeros_like(top)
        for at in range(0, count, chunk):
            part = slice(at, at + chunk)
            values = logits[k % 2, part, :]
            hit = lax.broadcasted_iota(jnp.int32, values.shape, 0) + at == targets[k][...]
            positive = positive + jnp.sum(jnp.where(hit, values, 0.0), axis=0, keepdims=True)
            e = jnp.exp(values - top)
            total = total + jnp.sum(e, axis=0, keepdims=True)
            e_outs[k][part, :] = e.astype(BF16)
        row_outs[k][0:1, :] = top
        row_outs[k][1:2, :] = positive
        log_sum = top + jnp.log(total)
        for b in range(4):
            slot = slot_of(k, b)
            lanes = slice(b * rows, (b + 1) * rows)
            stat[:, pl.ds(pl.multiple_of(slot * 128, 128), rows)] = jnp.broadcast_to(
                log_sum[:, lanes], (16, rows)
            )
            for_dest = jnp.where(dest == slot, positive[:, lanes], for_dest)
    stat[:, 2048 : 2048 + rows] = for_dest


def join_kernel(*refs):
    out = refs[-1]
    at = 0
    for part in refs[:-1]:
        size = min(part.shape[0], out.shape[0] - at)
        out[at : at + size, :] = part[:size, :]
        at += size


def delta_kernel(rows, chunk, stat, *refs):
    e_parts, row_parts, targets, deltas = refs[:4], refs[4:8], refs[8:12], refs[12:16]
    loss, totals, lane = refs[16:]
    count = e_parts[0].shape[0]
    sums = stat[:, :2048]
    top = jnp.max(sums, axis=0, keepdims=True)
    totals[0:1, :] = top + jnp.log(jnp.sum(jnp.exp(sums - top), axis=0, keepdims=True))
    own = totals[0:1, pl.ds(pl.multiple_of(slot_of(0, 0) * 128, 128), rows)]
    loss[...] = own - jnp.sum(stat[:, 2048:], axis=0, keepdims=True)[:, :rows]
    for k in range(4):
        for b in range(4):
            lane[k : k + 1, b * rows : (b + 1) * rows] = totals[
                0:1, pl.ds(pl.multiple_of(slot_of(k, b) * 128, 128), rows)
            ]
    for k in range(4):
        total = lane[k : k + 1, :]
        factor = jnp.exp(row_parts[k][0:1, :] - total)
        at_hit = jnp.exp(row_parts[k][1:2, :] - total) - 1.0
        for at in range(0, count, chunk):
            part = slice(at, at + chunk)
            prob = e_parts[k][part, :].astype(F32) * factor
            hit = lax.broadcasted_iota(jnp.int32, prob.shape, 0) + at == targets[k][...]
            deltas[k][part, :] = jnp.where(hit, at_hit, prob).astype(BF16)


def p_grads_kernel(first, temp, *refs):
    deltas, q_parts, outs = refs[:4], refs[4:8], refs[8:]
    at = first
    for out in outs:
        size = out.shape[0]
        total = jnp.zeros(out.shape, F32)
        for delta, q in zip(deltas, q_parts):
            total = total + jnp.dot(
                delta[at : at + size, :], q[...], preferred_element_type=F32
            )
        out[...] = (temp[0] * total).astype(BF16)
        at += size


def q_grads(scale, delta, p_all):
    return (
        scale
        * lax.dot_general(
            delta[...], p_all[...], (((0,), (0,)), ((), ())), preferred_element_type=F32
        )
    ).astype(BF16)


def q_grads_kernel(temp, delta, p_all, out):
    out[...] = q_grads(temp[0], delta, p_all)


def local_grads_kernel(temp, p_all, *refs):
    p_grads_kernel(0, temp, *refs[:-1])
    refs[-1][...] = q_grads(temp[0], refs[0], p_all)


def add_kernel(starts, *refs):
    terms, outs = refs[: len(starts)], refs[len(starts) :]
    at = 0
    for out in outs:
        size = out.shape[0]
        total = None
        for term, start in zip(terms, starts):
            if start + at + size > term.shape[0]:
                continue
            value = term[start + at : start + at + size, :].astype(F32)
            total = value if total is None else total + value
        out[...] = total.astype(out.dtype)
        at += size


def final_kernel(src, *refs):
    grad = refs[0][...].astype(F32)
    for ref in refs[1:-1]:
        grad = grad + ref[...].astype(F32)
    wide = src[...].astype(F32)
    length = jnp.sqrt(jnp.sum(wide * wide, axis=1, keepdims=True))
    unit = wide / length
    along = jnp.sum(unit * grad, axis=1, keepdims=True)
    refs[-1][...] = ((grad - unit * along) / length).astype(BF16)


def vmem(n):
    return [pl.BlockSpec(memory_space=pltpu.VMEM)] * n


def smem(n):
    return [pl.BlockSpec(memory_space=pltpu.SMEM)] * n


def call(kernel, shapes, in_specs, args, scratch=()):
    multi = isinstance(shapes, (list, tuple))
    return pl.pallas_call(
        kernel,
        out_shape=shapes,
        in_specs=in_specs,
        out_specs=vmem(len(shapes)) if multi else vmem(1)[0],
        scratch_shapes=list(scratch),
        compiler_params=pltpu.CompilerParams(vmem_limit_bytes=VMEM_LIMIT),
    )(*args)


def join(rows, *parts):
    return call(
        join_kernel,
        jax.ShapeDtypeStruct((rows, parts[0].shape[1]), BF16),
        vmem(len(parts)),
        parts,
    )


def after(array, *others):
    return lax.optimization_barrier((array, *others))[0]


def gather(q_low, p_low):
    rows = q_low.shape[0]
    pair = join(2 * rows, p_low, swap(p_low))
    near = join(4 * rows, q_low, *(inner(q_low, k) for k in (1, 2, 3)))
    one = along_z(pair, 1)
    two = along_z(pair, 2)
    near = after(near, pair)
    far = [outer(near, k) for k in (1, 2, 3)]
    relay = after(two, near)
    three = along_z(relay, 1)
    four = along_z(join(rows, relay), 2)
    one_b = swap(after(one, far[0]))
    two_b = swap(two)
    return [near, *far], [pair, one, two, three, four, swap(four), one_b, two_b, swap(three)]


def add(sizes, *terms):
    width = terms[0][0].shape[1]
    return call(
        functools.partial(add_kernel, [start for _, start in terms]),
        [jax.ShapeDtypeStruct((size, width), BF16) for size in sizes],
        vmem(len(terms)),
        [array for array, _ in terms],
    )


def scatter_queries(parts, rows):
    terms = [parts[0]] + [outer(parts[k], -k) for k in (1, 2, 3)]
    near = add([rows] * 4, *((term, 0) for term in terms))
    return [near[0]] + [inner(near[k], -k) for k in (1, 2, 3)]


def scatter_passages(pair, one, two, three, four, rest, rows):
    crossed = swap(rest)
    (three,) = add([2 * rows], (three, 0), (crossed, 5 * rows))
    (four,) = add([rows], (four, 0), (crossed, 0))
    from_three = along_z(three, -1)
    from_four = along_z(four, -2)
    (one,) = add([2 * rows], (one, 0), (crossed, rows))
    from_one = along_z(one, -1)
    two = add([rows] * 2, (two, 0), (crossed, 3 * rows), (from_three, 0), (from_four, 0))
    from_two = along_z(join(2 * rows, *two), -2)
    here, there = add([rows] * 2, (pair, 0), (from_one, 0), (from_two, 0))
    return here, swap(there)


def local(queries, passages, positives, inv_temp):
    rows, width = queries.shape
    count = rows * 16
    part_rows = 4 * rows
    chunk = 256
    shape = jax.ShapeDtypeStruct
    temp = inv_temp.reshape(1)
    p_low, q_low = (
        call(norm_kernel, shape((rows, width), BF16), vmem(1), (array,))
        for array in (passages, queries)
    )
    q_parts, p_parts = gather(q_low, p_low)
    targets = call(
        functools.partial(target_kernel, rows),
        [shape((1, part_rows), jnp.int32)] * 4,
        vmem(1),
        (positives.reshape(32, rows),),
    )
    p_all, stat, *found = call(
        functools.partial(logits_kernel, rows, chunk),
        [shape((count, width), BF16), shape((16, 17 * 128), F32)]
        + [shape((count, part_rows), BF16)] * 4
        + [shape((8, part_rows), F32)] * 4,
        smem(1) + vmem(17),
        (temp, *q_parts, *targets, *p_parts),
        [pltpu.VMEM((2, count, part_rows), F32)],
    )
    e_parts, row_parts = found[:4], found[4:]
    stats = lax.all_to_all(stat, ("y", "x"), 0, 0, tiled=True)

    *deltas, loss = call(
        functools.partial(delta_kernel, rows, chunk),
        [shape((count, part_rows), BF16)] * 4 + [shape((1, rows), F32)],
        vmem(13),
        (stats, *e_parts, *row_parts, *targets),
        [pltpu.VMEM((8, 16 * 128), F32), pltpu.VMEM((8, part_rows), F32)],
    )

    three, four, rest = call(
        functools.partial(p_grads_kernel, 6 * rows),
        [shape((size * rows, width), BF16) for size in (2, 1, 7)],
        smem(1) + vmem(8),
        (temp, *deltas, *q_parts),
    )
    sent = [
        call(q_grads_kernel, shape((part_rows, width), BF16), smem(1) + vmem(2), (temp, delta, p_all))
        for delta in deltas[1:]
    ]
    pair, one, two, own = call(
        local_grads_kernel,
        [shape((size * rows, width), BF16) for size in (2, 2, 2, 4)],
        smem(1) + vmem(9),
        (temp, p_all, *deltas, *q_parts),
    )
    q_terms = scatter_queries([own, *sent], rows)
    p_terms = scatter_passages(pair, one, two, three, four, rest, rows)
    query_grads, passage_grads = (
        call(final_kernel, shape((rows, width), BF16), vmem(1 + len(terms)), (array, *terms))
        for array, terms in ((queries, q_terms), (passages, p_terms))
    )
    return (loss.reshape(rows), query_grads, passage_grads)


def solution(mesh):
    fine = Mesh(mesh.devices.reshape(SIZES), AXES)
    return jax.shard_map(
        local,
        mesh=fine,
        in_specs=(P(AXES, None), P(AXES, None), P(("zl", "core")), P()),
        out_specs=(P(AXES), P(AXES, None), P(AXES, None)),
        check_vma=False,
    )
```

```python
import functools

import jax
import jax.numpy as jnp
from jax import lax
from jax.experimental import pallas as pl
from jax.experimental.pallas import tpu as pltpu
from jax.sharding import Mesh
from jax.sharding import PartitionSpec as P

AXES = ("zl", "core", "y", "x", "zh")
SIZES = (4, 2, 4, 4, 2)
VMEM_LIMIT = 24 * 2**20
F32 = jnp.float32
BF16 = jnp.bfloat16


def device_at(z, core, y, x):
    z, y, x = z % 8, y % 4, x % 4
    return ((((z % 4) * 2 + core) * 4 + y) * 4 + x) * 2 + z // 4


def fetch(array, source):
    pairs = []
    for z in range(8):
        for core in range(2):
            for y in range(4):
                for x in range(4):
                    pairs.append((device_at(*source(z, core, y, x)), device_at(z, core, y, x)))
    return lax.ppermute(array, AXES, pairs)


def swap(array):
    return fetch(array, lambda z, c, y, x: (z, 1 - c, y, x))


def along_z(array, k):
    return fetch(array, lambda z, c, y, x: (z + (k if c == 0 else -k), c, y, x))


def inner(array, k):
    return fetch(array, lambda z, c, y, x: (z, c, y, x + k) if c == 0 else (z, c, y + k, x))


def outer(array, k):
    return fetch(array, lambda z, c, y, x: (z, c, y + k, x) if c == 0 else (z, c, y, x + k))


def place():
    return tuple(lax.axis_index(name) for name in AXES)


def slot_of(k, b):
    _, core, y, x, _ = place()
    step_y = jnp.where(core == 0, k, b)
    step_x = jnp.where(core == 0, b, k)
    return lax.rem(y + step_y, 4) * 4 + lax.rem(x + step_x, 4)


def norm_kernel(src, dst):
    wide = src[...].astype(F32)
    length = jnp.sqrt(jnp.sum(wide * wide, axis=1, keepdims=True))
    dst[...] = (wide / length).astype(BF16)


def target_kernel(rows, positives, *outs):
    zl, core, y, x, zh = place()
    z = zh * 4 + zl
    for k, out in enumerate(outs):
        for b in range(4):
            wanted = positives[pl.ds(slot_of(k, b) * 2 + zh, 1), :]
            block = lax.div(wanted, rows)
            owner_z = lax.rem(block, 2) * 4 + lax.div(block, 64)
            other = (lax.rem(lax.div(block, 32), 2) != core).astype(jnp.int32)
            away = lax.rem(jnp.where(core == 0, owner_z - z, z - owner_z) + 8, 8)
            slot = jnp.where(
                away < 4,
                2 * away + other,
                jnp.where(away == 4, 8 + 7 * other, 9 + 2 * (7 - away) + 1 - other),
            )
            owner = lax.rem(lax.div(block, 8), 4) * 4 + lax.rem(lax.div(block, 2), 4)
            row = slot * rows + lax.rem(wanted, rows)
            out[:, b * rows : (b + 1) * rows] = jnp.where(owner == y * 4 + x, row, -1)


def logits_kernel(rows, chunk, temp, *refs):
    q_parts, targets, p_parts = refs[:4], refs[4:8], refs[8:15]
    p_all, stat, e_outs, row_outs, logits = refs[15], refs[16], refs[17:21], refs[21:25], refs[25]
    count = p_all.shape[0]
    scale = temp[0]
    at = 0
    for part in p_parts:
        p_all[at : at + part.shape[0], :] = part[...]
        at += part.shape[0]
    stat[...] = jnp.zeros_like(stat)
    dest = lax.broadcasted_iota(jnp.int32, (16, rows), 0)
    for_dest = jnp.zeros((16, rows), F32)
    for k in range(4):
        tops = []
        for at in range(0, count, chunk):
            part = slice(at, at + chunk)
            values = scale * lax.dot_general(
                p_all[part, :], q_parts[k][...], (((1,), (1,)), ((), ())), preferred_element_type=F32
            )
            logits[k % 2, part, :] = values
            tops.append(jnp.max(values, axis=0, keepdims=True))
        top = functools.reduce(jnp.maximum, tops)
        total = jnp.zeros_like(top)
        positive = jnp.zeros_like(top)
        for at in range(0, count, chunk):
            part = slice(at, at + chunk)
            values = logits[k % 2, part, :]
            hit = lax.broadcasted_iota(jnp.int32, values.shape, 0) + at == targets[k][...]
            positive = positive + jnp.sum(jnp.where(hit, values, 0.0), axis=0, keepdims=True)
            e = jnp.exp(values - top)
            total = total + jnp.sum(e, axis=0, keepdims=True)
            e_outs[k][part, :] = e.astype(BF16)
        row_outs[k][0:1, :] = top
        row_outs[k][1:2, :] = positive
        log_sum = top + jnp.log(total)
        for b in range(4):
            slot = slot_of(k, b)
            lanes = slice(b * rows, (b + 1) * rows)
            stat[:, pl.ds(pl.multiple_of(slot * 128, 128), rows)] = jnp.broadcast_to(
                log_sum[:, lanes], (16, rows)
            )
            for_dest = jnp.where(dest == slot, positive[:, lanes], for_dest)
    stat[:, 2048 : 2048 + rows] = for_dest


def join_kernel(*refs):
    out = refs[-1]
    at = 0
    for part in refs[:-1]:
        size = min(part.shape[0], out.shape[0] - at)
        out[at : at + size, :] = part[:size, :]
        at += size


def delta_kernel(rows, chunk, stat, *refs):
    e_parts, row_parts, targets, deltas = refs[:4], refs[4:8], refs[8:12], refs[12:16]
    loss, totals, lane = refs[16:]
    count = e_parts[0].shape[0]
    sums = stat[:, :2048]
    top = jnp.max(sums, axis=0, keepdims=True)
    totals[0:1, :] = top + jnp.log(jnp.sum(jnp.exp(sums - top), axis=0, keepdims=True))
    own = totals[0:1, pl.ds(pl.multiple_of(slot_of(0, 0) * 128, 128), rows)]
    loss[...] = own - jnp.sum(stat[:, 2048:], axis=0, keepdims=True)[:, :rows]
    for k in range(4):
        for b in range(4):
            lane[k : k + 1, b * rows : (b + 1) * rows] = totals[
                0:1, pl.ds(pl.multiple_of(slot_of(k, b) * 128, 128), rows)
            ]
    for k in range(4):
        total = lane[k : k + 1, :]
        factor = jnp.exp(row_parts[k][0:1, :] - total)
        at_hit = jnp.exp(row_parts[k][1:2, :] - total) - 1.0
        for at in range(0, count, chunk):
            part = slice(at, at + chunk)
            prob = e_parts[k][part, :].astype(F32) * factor
            hit = lax.broadcasted_iota(jnp.int32, prob.shape, 0) + at == targets[k][...]
            deltas[k][part, :] = jnp.where(hit, at_hit, prob).astype(BF16)


def p_grads_kernel(first, temp, *refs):
    deltas, q_parts, outs = refs[:4], refs[4:8], refs[8:]
    at = first
    for out in outs:
        size = out.shape[0]
        total = jnp.zeros(out.shape, F32)
        for delta, q in zip(deltas, q_parts):
            total = total + jnp.dot(
                delta[at : at + size, :], q[...], preferred_element_type=F32
            )
        out[...] = (temp[0] * total).astype(BF16)
        at += size


def q_grads(scale, delta, p_all):
    return (
        scale
        * lax.dot_general(
            delta[...], p_all[...], (((0,), (0,)), ((), ())), preferred_element_type=F32
        )
    ).astype(BF16)


def q_grads_kernel(temp, delta, p_all, out):
    out[...] = q_grads(temp[0], delta, p_all)


def local_grads_kernel(temp, p_all, *refs):
    p_grads_kernel(0, temp, *refs[:-1])
    refs[-1][...] = q_grads(temp[0], refs[0], p_all)


def add_kernel(starts, *refs):
    terms, outs = refs[: len(starts)], refs[len(starts) :]
    at = 0
    for out in outs:
        size = out.shape[0]
        total = None
        for term, start in zip(terms, starts):
            if start + at + size > term.shape[0]:
                continue
            value = term[start + at : start + at + size, :].astype(F32)
            total = value if total is None else total + value
        out[...] = total.astype(out.dtype)
        at += size


def final_kernel(src, *refs):
    grad = refs[0][...].astype(F32)
    for ref in refs[1:-1]:
        grad = grad + ref[...].astype(F32)
    wide = src[...].astype(F32)
    length = jnp.sqrt(jnp.sum(wide * wide, axis=1, keepdims=True))
    unit = wide / length
    along = jnp.sum(unit * grad, axis=1, keepdims=True)
    refs[-1][...] = ((grad - unit * along) / length).astype(BF16)


def vmem(n):
    return [pl.BlockSpec(memory_space=pltpu.VMEM)] * n


def smem(n):
    return [pl.BlockSpec(memory_space=pltpu.SMEM)] * n


def call(kernel, shapes, in_specs, args, scratch=()):
    multi = isinstance(shapes, (list, tuple))
    return pl.pallas_call(
        kernel,
        out_shape=shapes,
        in_specs=in_specs,
        out_specs=vmem(len(shapes)) if multi else vmem(1)[0],
        scratch_shapes=list(scratch),
        compiler_params=pltpu.CompilerParams(vmem_limit_bytes=VMEM_LIMIT),
    )(*args)


def join(rows, *parts):
    return call(
        join_kernel,
        jax.ShapeDtypeStruct((rows, parts[0].shape[1]), BF16),
        vmem(len(parts)),
        parts,
    )


def after(array, *others):
    return lax.optimization_barrier((array, *others))[0]


def gather(q_low, p_low):
    rows = q_low.shape[0]
    pair = join(2 * rows, p_low, swap(p_low))
    near = join(4 * rows, q_low, *(inner(q_low, k) for k in (1, 2, 3)))
    two = along_z(pair, 2)
    near = after(near, pair)
    far = [outer(near, k) for k in (1, 2, 3)]
    relay = after(two, near)
    one = along_z(after(pair, relay), 1)
    three = along_z(relay, 1)
    four = along_z(join(rows, relay), 2)
    one_b = swap(after(one, far[0], far[2]))
    two_b = swap(after(two, far[1]))
    last = join(3 * rows, three, four)
    return [near, *far], [pair, one, two, last, one_b, two_b, swap(last)]


def add(sizes, *terms):
    width = terms[0][0].shape[1]
    return call(
        functools.partial(add_kernel, [start for _, start in terms]),
        [jax.ShapeDtypeStruct((size, width), BF16) for size in sizes],
        vmem(len(terms)),
        [array for array, _ in terms],
    )


def scatter_queries(parts, rows):
    terms = [parts[0]] + [outer(parts[k], -k) for k in (1, 2, 3)]
    near = add([rows] * 4, *((term, 0) for term in terms))
    return [near[0]] + [inner(near[k], -k) for k in (1, 2, 3)]


def scatter_passages(pair, one, two, three, four, rest, rows):
    crossed = swap(rest)
    (three,) = add([2 * rows], (three, 0), (crossed, 4 * rows))
    (four,) = add([rows], (four, 0), (crossed, 6 * rows))
    from_three = along_z(three, -1)
    from_four = along_z(four, -2)
    (one,) = add([2 * rows], (one, 0), (crossed, 0))
    from_one = along_z(one, -1)
    two = add([rows] * 2, (two, 0), (crossed, 2 * rows), (from_three, 0), (from_four, 0))
    from_two = along_z(join(2 * rows, *two), -2)
    here, there = add([rows] * 2, (pair, 0), (from_one, 0), (from_two, 0))
    return here, swap(there)


def local(queries, passages, positives, inv_temp):
    rows, width = queries.shape
    count = rows * 16
    part_rows = 4 * rows
    chunk = 256
    shape = jax.ShapeDtypeStruct
    temp = inv_temp.reshape(1)
    p_low, q_low = (
        call(norm_kernel, shape((rows, width), BF16), vmem(1), (array,))
        for array in (passages, queries)
    )
    q_parts, p_parts = gather(q_low, p_low)
    targets = call(
        functools.partial(target_kernel, rows),
        [shape((1, part_rows), jnp.int32)] * 4,
        vmem(1),
        (positives.reshape(32, rows),),
    )
    p_all, stat, *found = call(
        functools.partial(logits_kernel, rows, chunk),
        [shape((count, width), BF16), shape((16, 17 * 128), F32)]
        + [shape((count, part_rows), BF16)] * 4
        + [shape((8, part_rows), F32)] * 4,
        smem(1) + vmem(15),
        (temp, *q_parts, *targets, *p_parts),
        [pltpu.VMEM((2, count, part_rows), F32)],
    )
    e_parts, row_parts = found[:4], found[4:]
    stats = lax.all_to_all(stat, ("y", "x"), 0, 0, tiled=True)

    *deltas, loss = call(
        functools.partial(delta_kernel, rows, chunk),
        [shape((count, part_rows), BF16)] * 4 + [shape((1, rows), F32)],
        vmem(13),
        (stats, *e_parts, *row_parts, *targets),
        [pltpu.VMEM((8, 16 * 128), F32), pltpu.VMEM((8, part_rows), F32)],
    )

    three, four, rest = call(
        functools.partial(p_grads_kernel, 6 * rows),
        [shape((size * rows, width), BF16) for size in (2, 1, 7)],
        smem(1) + vmem(8),
        (temp, *deltas, *q_parts),
    )
    sent = [
        call(q_grads_kernel, shape((part_rows, width), BF16), smem(1) + vmem(2), (temp, delta, p_all))
        for delta in deltas[1:]
    ]
    pair, one, two, own = call(
        local_grads_kernel,
        [shape((size * rows, width), BF16) for size in (2, 2, 2, 4)],
        smem(1) + vmem(9),
        (temp, p_all, *deltas, *q_parts),
    )
    q_terms = scatter_queries([own, *sent], rows)
    p_terms = scatter_passages(pair, one, two, three, four, rest, rows)
    query_grads, passage_grads = (
        call(final_kernel, shape((rows, width), BF16), vmem(1 + len(terms)), (array, *terms))
        for array, terms in ((queries, q_terms), (passages, p_terms))
    )
    return (loss.reshape(rows), query_grads, passage_grads)


def solution(mesh):
    fine = Mesh(mesh.devices.reshape(SIZES), AXES)
    return jax.shard_map(
        local,
        mesh=fine,
        in_specs=(P(AXES, None), P(AXES, None), P(("zl", "core")), P()),
        out_specs=(P(AXES), P(AXES, None), P(AXES, None)),
        check_vma=False,
    )
```

```python
import functools

import jax
import jax.numpy as jnp
from jax import lax
from jax.experimental import pallas as pl
from jax.experimental.pallas import tpu as pltpu
from jax.sharding import Mesh
from jax.sharding import PartitionSpec as P

AXES = ("zl", "core", "y", "x", "zh")
SIZES = (4, 2, 4, 4, 2)
VMEM_LIMIT = 24 * 2**20
F32 = jnp.float32
BF16 = jnp.bfloat16


def device_at(z, core, y, x):
    z, y, x = z % 8, y % 4, x % 4
    return ((((z % 4) * 2 + core) * 4 + y) * 4 + x) * 2 + z // 4


def fetch(array, source):
    pairs = []
    for z in range(8):
        for core in range(2):
            for y in range(4):
                for x in range(4):
                    pairs.append((device_at(*source(z, core, y, x)), device_at(z, core, y, x)))
    return lax.ppermute(array, AXES, pairs)


def swap(array):
    return fetch(array, lambda z, c, y, x: (z, 1 - c, y, x))


def along_z(array, k):
    return fetch(array, lambda z, c, y, x: (z + (k if c == 0 else -k), c, y, x))


def inner(array, k):
    return fetch(array, lambda z, c, y, x: (z, c, y, x + k) if c == 0 else (z, c, y + k, x))


def outer(array, k):
    return fetch(array, lambda z, c, y, x: (z, c, y + k, x) if c == 0 else (z, c, y, x + k))


def place():
    return tuple(lax.axis_index(name) for name in AXES)


def slot_of(k, b):
    _, core, y, x, _ = place()
    step_y = jnp.where(core == 0, k, b)
    step_x = jnp.where(core == 0, b, k)
    return lax.rem(y + step_y, 4) * 4 + lax.rem(x + step_x, 4)


def norm_kernel(src, dst):
    wide = src[...].astype(F32)
    length = jnp.sqrt(jnp.sum(wide * wide, axis=1, keepdims=True))
    dst[...] = (wide / length).astype(BF16)


def target_kernel(rows, positives, *outs):
    zl, core, y, x, zh = place()
    z = zh * 4 + zl
    for k, out in enumerate(outs):
        for b in range(4):
            wanted = positives[pl.ds(slot_of(k, b) * 2 + zh, 1), :]
            block = lax.div(wanted, rows)
            owner_z = lax.rem(block, 2) * 4 + lax.div(block, 64)
            other = (lax.rem(lax.div(block, 32), 2) != core).astype(jnp.int32)
            away = lax.rem(jnp.where(core == 0, owner_z - z, z - owner_z) + 8, 8)
            slot = jnp.where(
                away < 4,
                2 * away + other,
                jnp.where(away == 4, 8 + other, 10 + 2 * (7 - away) + 1 - other),
            )
            owner = lax.rem(lax.div(block, 8), 4) * 4 + lax.rem(lax.div(block, 2), 4)
            row = slot * rows + lax.rem(wanted, rows)
            out[:, b * rows : (b + 1) * rows] = jnp.where(owner == y * 4 + x, row, -1)


def logits_kernel(rows, chunk, temp, *refs):
    q_parts, targets, p_parts = refs[:4], refs[4:8], refs[8:17]
    p_all, stat, e_outs, row_outs, logits = refs[17], refs[18], refs[19:23], refs[23:27], refs[27]
    count = p_all.shape[0]
    scale = temp[0]
    at = 0
    for part in p_parts:
        p_all[at : at + part.shape[0], :] = part[...]
        at += part.shape[0]
    stat[...] = jnp.zeros_like(stat)
    dest = lax.broadcasted_iota(jnp.int32, (16, rows), 0)
    for_dest = jnp.zeros((16, rows), F32)
    for k in range(4):
        tops = []
        for at in range(0, count, chunk):
            part = slice(at, at + chunk)
            values = scale * lax.dot_general(
                p_all[part, :], q_parts[k][...], (((1,), (1,)), ((), ())), preferred_element_type=F32
            )
            logits[k % 2, part, :] = values
            tops.append(jnp.max(values, axis=0, keepdims=True))
        top = functools.reduce(jnp.maximum, tops)
        total = jnp.zeros_like(top)
        positive = jnp.zeros_like(top)
        for at in range(0, count, chunk):
            part = slice(at, at + chunk)
            values = logits[k % 2, part, :]
            hit = lax.broadcasted_iota(jnp.int32, values.shape, 0) + at == targets[k][...]
            positive = positive + jnp.sum(jnp.where(hit, values, 0.0), axis=0, keepdims=True)
            e = jnp.exp(values - top)
            total = total + jnp.sum(e, axis=0, keepdims=True)
            e_outs[k][part, :] = e.astype(BF16)
        row_outs[k][0:1, :] = top
        row_outs[k][1:2, :] = positive
        log_sum = top + jnp.log(total)
        for b in range(4):
            slot = slot_of(k, b)
            lanes = slice(b * rows, (b + 1) * rows)
            stat[:, pl.ds(pl.multiple_of(slot * 128, 128), rows)] = jnp.broadcast_to(
                log_sum[:, lanes], (16, rows)
            )
            for_dest = jnp.where(dest == slot, positive[:, lanes], for_dest)
    stat[:, 2048 : 2048 + rows] = for_dest


def join_kernel(*refs):
    out = refs[-1]
    at = 0
    for part in refs[:-1]:
        size = min(part.shape[0], out.shape[0] - at)
        out[at : at + size, :] = part[:size, :]
        at += size


def delta_kernel(rows, chunk, stat, *refs):
    e_parts, row_parts, targets, deltas = refs[:4], refs[4:8], refs[8:12], refs[12:16]
    loss, totals, lane = refs[16:]
    count = e_parts[0].shape[0]
    sums = stat[:, :2048]
    top = jnp.max(sums, axis=0, keepdims=True)
    totals[0:1, :] = top + jnp.log(jnp.sum(jnp.exp(sums - top), axis=0, keepdims=True))
    own = totals[0:1, pl.ds(pl.multiple_of(slot_of(0, 0) * 128, 128), rows)]
    loss[...] = own - jnp.sum(stat[:, 2048:], axis=0, keepdims=True)[:, :rows]
    for k in range(4):
        for b in range(4):
            lane[k : k + 1, b * rows : (b + 1) * rows] = totals[
                0:1, pl.ds(pl.multiple_of(slot_of(k, b) * 128, 128), rows)
            ]
    for k in range(4):
        total = lane[k : k + 1, :]
        factor = jnp.exp(row_parts[k][0:1, :] - total)
        at_hit = jnp.exp(row_parts[k][1:2, :] - total) - 1.0
        for at in range(0, count, chunk):
            part = slice(at, at + chunk)
            prob = e_parts[k][part, :].astype(F32) * factor
            hit = lax.broadcasted_iota(jnp.int32, prob.shape, 0) + at == targets[k][...]
            deltas[k][part, :] = jnp.where(hit, at_hit, prob).astype(BF16)


def p_grads_kernel(first, temp, *refs):
    deltas, q_parts, outs = refs[:4], refs[4:8], refs[8:]
    end = first + sum(out.shape[0] for out in outs)
    total = None
    for delta, q in zip(deltas, q_parts):
        term = jnp.dot(delta[first:end, :], q[...], preferred_element_type=F32)
        total = term if total is None else total + term
    low = (temp[0] * total).astype(BF16)
    at = 0
    for out in outs:
        size = out.shape[0]
        out[...] = low[at : at + size, :]
        at += size


def q_grads(scale, delta, p_all):
    return (
        scale
        * lax.dot_general(
            delta[...], p_all[...], (((0,), (0,)), ((), ())), preferred_element_type=F32
        )
    ).astype(BF16)


def q_grads_kernel(temp, delta, p_all, out):
    out[...] = q_grads(temp[0], delta, p_all)


def local_grads_kernel(temp, p_all, *refs):
    p_grads_kernel(0, temp, *refs[:-1])
    refs[-1][...] = q_grads(temp[0], refs[0], p_all)


def add_kernel(starts, *refs):
    terms, outs = refs[: len(starts)], refs[len(starts) :]
    at = 0
    for out in outs:
        size = out.shape[0]
        total = None
        for term, start in zip(terms, starts):
            if start + at + size > term.shape[0]:
                continue
            value = term[start + at : start + at + size, :].astype(F32)
            total = value if total is None else total + value
        out[...] = total.astype(out.dtype)
        at += size


def final_kernel(src, *refs):
    grad = refs[0][...].astype(F32)
    for ref in refs[1:-1]:
        grad = grad + ref[...].astype(F32)
    wide = src[...].astype(F32)
    length = jnp.sqrt(jnp.sum(wide * wide, axis=1, keepdims=True))
    unit = wide / length
    along = jnp.sum(unit * grad, axis=1, keepdims=True)
    refs[-1][...] = ((grad - unit * along) / length).astype(BF16)


def vmem(n):
    return [pl.BlockSpec(memory_space=pltpu.VMEM)] * n


def smem(n):
    return [pl.BlockSpec(memory_space=pltpu.SMEM)] * n


def call(kernel, shapes, in_specs, args, scratch=()):
    multi = isinstance(shapes, (list, tuple))
    return pl.pallas_call(
        kernel,
        out_shape=shapes,
        in_specs=in_specs,
        out_specs=vmem(len(shapes)) if multi else vmem(1)[0],
        scratch_shapes=list(scratch),
        compiler_params=pltpu.CompilerParams(vmem_limit_bytes=VMEM_LIMIT),
    )(*args)


def join(rows, *parts):
    return call(
        join_kernel,
        jax.ShapeDtypeStruct((rows, parts[0].shape[1]), BF16),
        vmem(len(parts)),
        parts,
    )


def after(array, *others):
    return lax.optimization_barrier((array, *others))[0]


def gather(q_low, p_low):
    rows = q_low.shape[0]
    pair = join(2 * rows, p_low, swap(p_low))
    near = join(4 * rows, q_low, *(inner(q_low, k) for k in (1, 2, 3)))
    one = along_z(pair, 1)
    two = along_z(pair, 2)
    near = after(near, pair)
    far = [outer(near, k) for k in (1, 2, 3)]
    relay = after(two, near)
    three = along_z(relay, 1)
    four = along_z(join(rows, relay), 2)
    one_b = swap(after(one, far[0]))
    two_b = swap(two)
    return [near, *far], [pair, one, two, three, four, swap(four), one_b, two_b, swap(three)]


def add(sizes, *terms):
    width = terms[0][0].shape[1]
    return call(
        functools.partial(add_kernel, [start for _, start in terms]),
        [jax.ShapeDtypeStruct((size, width), BF16) for size in sizes],
        vmem(len(terms)),
        [array for array, _ in terms],
    )


def scatter_queries(parts, rows):
    terms = [parts[0]] + [outer(parts[k], -k) for k in (1, 2, 3)]
    near = add([rows] * 4, *((term, 0) for term in terms))
    return [near[0]] + [inner(near[k], -k) for k in (1, 2, 3)]


def scatter_passages(pair, one, two, three, four, rest, rows):
    crossed = swap(rest)
    (three,) = add([2 * rows], (three, 0), (crossed, 5 * rows))
    (four,) = add([rows], (four, 0), (crossed, 0))
    from_three = along_z(three, -1)
    from_four = along_z(four, -2)
    (one,) = add([2 * rows], (one, 0), (crossed, rows))
    from_one = along_z(one, -1)
    two = add([rows] * 2, (two, 0), (crossed, 3 * rows), (from_three, 0), (from_four, 0))
    from_two = along_z(join(2 * rows, *two), -2)
    here, there = add([rows] * 2, (pair, 0), (from_one, 0), (from_two, 0))
    return here, swap(there)


def local(queries, passages, positives, inv_temp):
    rows, width = queries.shape
    count = rows * 16
    part_rows = 4 * rows
    chunk = 256
    shape = jax.ShapeDtypeStruct
    temp = inv_temp.reshape(1)
    p_low, q_low = (
        call(norm_kernel, shape((rows, width), BF16), vmem(1), (array,))
        for array in (passages, queries)
    )
    q_parts, p_parts = gather(q_low, p_low)
    targets = call(
        functools.partial(target_kernel, rows),
        [shape((1, part_rows), jnp.int32)] * 4,
        vmem(1),
        (positives.reshape(32, rows),),
    )
    p_all, stat, *found = call(
        functools.partial(logits_kernel, rows, chunk),
        [shape((count, width), BF16), shape((16, 17 * 128), F32)]
        + [shape((count, part_rows), BF16)] * 4
        + [shape((8, part_rows), F32)] * 4,
        smem(1) + vmem(17),
        (temp, *q_parts, *targets, *p_parts),
        [pltpu.VMEM((2, count, part_rows), F32)],
    )
    e_parts, row_parts = found[:4], found[4:]
    stats = lax.all_to_all(stat, ("y", "x"), 0, 0, tiled=True)

    *deltas, loss = call(
        functools.partial(delta_kernel, rows, chunk),
        [shape((count, part_rows), BF16)] * 4 + [shape((1, rows), F32)],
        vmem(13),
        (stats, *e_parts, *row_parts, *targets),
        [pltpu.VMEM((8, 16 * 128), F32), pltpu.VMEM((8, part_rows), F32)],
    )

    three, four, rest = call(
        functools.partial(p_grads_kernel, 6 * rows),
        [shape((size * rows, width), BF16) for size in (2, 1, 7)],
        smem(1) + vmem(8),
        (temp, *deltas, *q_parts),
    )
    sent = [
        call(q_grads_kernel, shape((part_rows, width), BF16), smem(1) + vmem(2), (temp, delta, p_all))
        for delta in deltas[1:]
    ]
    pair, one, two, own = call(
        local_grads_kernel,
        [shape((size * rows, width), BF16) for size in (2, 2, 2, 4)],
        smem(1) + vmem(9),
        (temp, p_all, *deltas, *q_parts),
    )
    q_terms = scatter_queries([own, *sent], rows)
    p_terms = scatter_passages(pair, one, two, three, four, rest, rows)
    query_grads, passage_grads = (
        call(final_kernel, shape((rows, width), BF16), vmem(1 + len(terms)), (array, *terms))
        for array, terms in ((queries, q_terms), (passages, p_terms))
    )
    return (loss.reshape(rows), query_grads, passage_grads)


def solution(mesh):
    fine = Mesh(mesh.devices.reshape(SIZES), AXES)
    return jax.shard_map(
        local,
        mesh=fine,
        in_specs=(P(AXES, None), P(AXES, None), P(("zl", "core")), P()),
        out_specs=(P(AXES), P(AXES, None), P(AXES, None)),
        check_vma=False,
    )
```

```python
import functools

import jax
import jax.numpy as jnp
from jax import lax
from jax.experimental import pallas as pl
from jax.experimental.pallas import tpu as pltpu
from jax.sharding import Mesh
from jax.sharding import PartitionSpec as P

AXES = ("zl", "core", "y", "x", "zh")
SIZES = (4, 2, 4, 4, 2)
VMEM_LIMIT = 24 * 2**20
F32 = jnp.float32
BF16 = jnp.bfloat16


def device_at(z, core, y, x):
    z, y, x = z % 8, y % 4, x % 4
    return ((((z % 4) * 2 + core) * 4 + y) * 4 + x) * 2 + z // 4


def fetch(array, source):
    pairs = []
    for z in range(8):
        for core in range(2):
            for y in range(4):
                for x in range(4):
                    pairs.append((device_at(*source(z, core, y, x)), device_at(z, core, y, x)))
    return lax.ppermute(array, AXES, pairs)


def swap(array):
    return fetch(array, lambda z, c, y, x: (z, 1 - c, y, x))


def along_z(array, k):
    return fetch(array, lambda z, c, y, x: (z + (k if c == 0 else -k), c, y, x))


def inner(array, k):
    return fetch(array, lambda z, c, y, x: (z, c, y, x + k) if c == 0 else (z, c, y + k, x))


def outer(array, k):
    return fetch(array, lambda z, c, y, x: (z, c, y + k, x) if c == 0 else (z, c, y, x + k))


def place():
    return tuple(lax.axis_index(name) for name in AXES)


def slot_of(k, b):
    _, core, y, x, _ = place()
    step_y = jnp.where(core == 0, k, b)
    step_x = jnp.where(core == 0, b, k)
    return lax.rem(y + step_y, 4) * 4 + lax.rem(x + step_x, 4)


def norm_kernel(src, dst):
    wide = src[...].astype(F32)
    length = jnp.sqrt(jnp.sum(wide * wide, axis=1, keepdims=True))
    dst[...] = (wide / length).astype(BF16)


def target_kernel(rows, positives, *outs):
    zl, core, y, x, zh = place()
    z = zh * 4 + zl
    for k, out in enumerate(outs):
        for b in range(4):
            wanted = positives[pl.ds(slot_of(k, b) * 2 + zh, 1), :]
            block = lax.div(wanted, rows)
            owner_z = lax.rem(block, 2) * 4 + lax.div(block, 64)
            other = (lax.rem(lax.div(block, 32), 2) != core).astype(jnp.int32)
            away = lax.rem(jnp.where(core == 0, owner_z - z, z - owner_z) + 8, 8)
            slot = jnp.where(
                away < 4,
                2 * away + other,
                jnp.where(away == 4, 8 + other, 10 + 2 * (7 - away) + 1 - other),
            )
            owner = lax.rem(lax.div(block, 8), 4) * 4 + lax.rem(lax.div(block, 2), 4)
            row = slot * rows + lax.rem(wanted, rows)
            out[:, b * rows : (b + 1) * rows] = jnp.where(owner == y * 4 + x, row, -1)


def logits_kernel(rows, chunk, temp, *refs):
    q_parts, targets, p_parts = refs[:4], refs[4:8], refs[8:16]
    p_all, stat, e_outs, row_outs, logits = refs[16], refs[17], refs[18:22], refs[22:26], refs[26]
    count = p_all.shape[0]
    scale = temp[0]
    at = 0
    for part in p_parts:
        p_all[at : at + part.shape[0], :] = part[...]
        at += part.shape[0]
    stat[...] = jnp.zeros_like(stat)
    dest = lax.broadcasted_iota(jnp.int32, (16, rows), 0)
    for_dest = jnp.zeros((16, rows), F32)
    for k in range(4):
        tops = []
        for at in range(0, count, chunk):
            part = slice(at, at + chunk)
            values = scale * lax.dot_general(
                p_all[part, :], q_parts[k][...], (((1,), (1,)), ((), ())), preferred_element_type=F32
            )
            logits[k % 2, part, :] = values
            tops.append(jnp.max(values, axis=0, keepdims=True))
        top = functools.reduce(jnp.maximum, tops)
        total = jnp.zeros_like(top)
        positive = jnp.zeros_like(top)
        for at in range(0, count, chunk):
            part = slice(at, at + chunk)
            values = logits[k % 2, part, :]
            hit = lax.broadcasted_iota(jnp.int32, values.shape, 0) + at == targets[k][...]
            positive = positive + jnp.sum(jnp.where(hit, values, 0.0), axis=0, keepdims=True)
            e = jnp.exp(values - top)
            total = total + jnp.sum(e, axis=0, keepdims=True)
            e_outs[k][part, :] = e.astype(BF16)
        row_outs[k][0:1, :] = top
        row_outs[k][1:2, :] = positive
        log_sum = top + jnp.log(total)
        for b in range(4):
            slot = slot_of(k, b)
            lanes = slice(b * rows, (b + 1) * rows)
            stat[:, pl.ds(pl.multiple_of(slot * 128, 128), rows)] = jnp.broadcast_to(
                log_sum[:, lanes], (16, rows)
            )
            for_dest = jnp.where(dest == slot, positive[:, lanes], for_dest)
    stat[:, 2048 : 2048 + rows] = for_dest


def join_kernel(*refs):
    out = refs[-1]
    at = 0
    for part in refs[:-1]:
        size = min(part.shape[0], out.shape[0] - at)
        out[at : at + size, :] = part[:size, :]
        at += size


def delta_kernel(rows, chunk, stat, *refs):
    e_parts, row_parts, targets, deltas = refs[:4], refs[4:8], refs[8:12], refs[12:16]
    loss, totals, lane = refs[16:]
    count = e_parts[0].shape[0]
    sums = stat[:, :2048]
    top = jnp.max(sums, axis=0, keepdims=True)
    totals[0:1, :] = top + jnp.log(jnp.sum(jnp.exp(sums - top), axis=0, keepdims=True))
    own = totals[0:1, pl.ds(pl.multiple_of(slot_of(0, 0) * 128, 128), rows)]
    loss[...] = own - jnp.sum(stat[:, 2048:], axis=0, keepdims=True)[:, :rows]
    for k in range(4):
        for b in range(4):
            lane[k : k + 1, b * rows : (b + 1) * rows] = totals[
                0:1, pl.ds(pl.multiple_of(slot_of(k, b) * 128, 128), rows)
            ]
    for k in range(4):
        total = lane[k : k + 1, :]
        factor = jnp.exp(row_parts[k][0:1, :] - total)
        at_hit = jnp.exp(row_parts[k][1:2, :] - total) - 1.0
        for at in range(0, count, chunk):
            part = slice(at, at + chunk)
            prob = e_parts[k][part, :].astype(F32) * factor
            hit = lax.broadcasted_iota(jnp.int32, prob.shape, 0) + at == targets[k][...]
            deltas[k][part, :] = jnp.where(hit, at_hit, prob).astype(BF16)


def p_grads_kernel(first, temp, *refs):
    deltas, q_parts, outs = refs[:4], refs[4:8], refs[8:]
    at = first
    for out in outs:
        size = out.shape[0]
        total = jnp.zeros(out.shape, F32)
        for delta, q in zip(deltas, q_parts):
            total = total + jnp.dot(
                delta[at : at + size, :], q[...], preferred_element_type=F32
            )
        out[...] = (temp[0] * total).astype(BF16)
        at += size


def q_grads(scale, delta, p_all):
    return (
        scale
        * lax.dot_general(
            delta[...], p_all[...], (((0,), (0,)), ((), ())), preferred_element_type=F32
        )
    ).astype(BF16)


def q_grads_kernel(temp, delta, p_all, out):
    out[...] = q_grads(temp[0], delta, p_all)


def local_grads_kernel(temp, p_all, *refs):
    p_grads_kernel(0, temp, *refs[:-1])
    refs[-1][...] = q_grads(temp[0], refs[0], p_all)


def add_kernel(starts, *refs):
    terms, outs = refs[: len(starts)], refs[len(starts) :]
    at = 0
    for out in outs:
        size = out.shape[0]
        total = None
        for term, start in zip(terms, starts):
            if start + at + size > term.shape[0]:
                continue
            value = term[start + at : start + at + size, :].astype(F32)
            total = value if total is None else total + value
        out[...] = total.astype(out.dtype)
        at += size


def final_kernel(src, *refs):
    grad = refs[0][...].astype(F32)
    for ref in refs[1:-1]:
        grad = grad + ref[...].astype(F32)
    wide = src[...].astype(F32)
    length = jnp.sqrt(jnp.sum(wide * wide, axis=1, keepdims=True))
    unit = wide / length
    along = jnp.sum(unit * grad, axis=1, keepdims=True)
    refs[-1][...] = ((grad - unit * along) / length).astype(BF16)


def vmem(n):
    return [pl.BlockSpec(memory_space=pltpu.VMEM)] * n


def smem(n):
    return [pl.BlockSpec(memory_space=pltpu.SMEM)] * n


def call(kernel, shapes, in_specs, args, scratch=()):
    multi = isinstance(shapes, (list, tuple))
    return pl.pallas_call(
        kernel,
        out_shape=shapes,
        in_specs=in_specs,
        out_specs=vmem(len(shapes)) if multi else vmem(1)[0],
        scratch_shapes=list(scratch),
        compiler_params=pltpu.CompilerParams(vmem_limit_bytes=VMEM_LIMIT),
    )(*args)


def join(rows, *parts):
    return call(
        join_kernel,
        jax.ShapeDtypeStruct((rows, parts[0].shape[1]), BF16),
        vmem(len(parts)),
        parts,
    )


def after(array, *others):
    return lax.optimization_barrier((array, *others))[0]


def gather(q_low, p_low):
    rows = q_low.shape[0]
    pair = join(2 * rows, p_low, swap(p_low))
    near = join(4 * rows, q_low, *(inner(q_low, k) for k in (1, 2, 3)))
    one = along_z(pair, 1)
    two = along_z(pair, 2)
    near = after(near, pair)
    far = [outer(near, k) for k in (1, 2, 3)]
    relay = after(two, near)
    three = along_z(relay, 1)
    four = along_z(join(rows, relay), 2)
    one_b = swap(after(one, far[0]))
    two_b = swap(two)
    fours = join(2 * rows, four, swap(four))
    three_b = swap(three)
    return [near, *far], [pair, one, two, three, fours, one_b, two_b, three_b]


def add(sizes, *terms):
    width = terms[0][0].shape[1]
    return call(
        functools.partial(add_kernel, [start for _, start in terms]),
        [jax.ShapeDtypeStruct((size, width), BF16) for size in sizes],
        vmem(len(terms)),
        [array for array, _ in terms],
    )


def scatter_queries(parts, rows):
    terms = [parts[0]] + [outer(parts[k], -k) for k in (1, 2, 3)]
    near = add([rows] * 4, *((term, 0) for term in terms))
    return [near[0]] + [inner(near[k], -k) for k in (1, 2, 3)]


def scatter_passages(pair, one, two, three, four, rest, rows):
    crossed = swap(rest)
    (three,) = add([2 * rows], (three, 0), (crossed, 5 * rows))
    (four,) = add([rows], (four, 0), (crossed, 0))
    from_three = along_z(three, -1)
    from_four = along_z(four, -2)
    (one,) = add([2 * rows], (one, 0), (crossed, rows))
    from_one = along_z(one, -1)
    two = add([rows] * 2, (two, 0), (crossed, 3 * rows), (from_three, 0), (from_four, 0))
    from_two = along_z(join(2 * rows, *two), -2)
    here, there = add([rows] * 2, (pair, 0), (from_one, 0), (from_two, 0))
    return here, swap(there)


def local(queries, passages, positives, inv_temp):
    rows, width = queries.shape
    count = rows * 16
    part_rows = 4 * rows
    chunk = 256
    shape = jax.ShapeDtypeStruct
    temp = inv_temp.reshape(1)
    p_low, q_low = (
        call(norm_kernel, shape((rows, width), BF16), vmem(1), (array,))
        for array in (passages, queries)
    )
    q_parts, p_parts = gather(q_low, p_low)
    targets = call(
        functools.partial(target_kernel, rows),
        [shape((1, part_rows), jnp.int32)] * 4,
        vmem(1),
        (positives.reshape(32, rows),),
    )
    p_all, stat, *found = call(
        functools.partial(logits_kernel, rows, chunk),
        [shape((count, width), BF16), shape((16, 17 * 128), F32)]
        + [shape((count, part_rows), BF16)] * 4
        + [shape((8, part_rows), F32)] * 4,
        smem(1) + vmem(16),
        (temp, *q_parts, *targets, *p_parts),
        [pltpu.VMEM((2, count, part_rows), F32)],
    )
    e_parts, row_parts = found[:4], found[4:]
    stats = lax.all_to_all(stat, ("y", "x"), 0, 0, tiled=True)

    *deltas, loss = call(
        functools.partial(delta_kernel, rows, chunk),
        [shape((count, part_rows), BF16)] * 4 + [shape((1, rows), F32)],
        vmem(13),
        (stats, *e_parts, *row_parts, *targets),
        [pltpu.VMEM((8, 16 * 128), F32), pltpu.VMEM((8, part_rows), F32)],
    )

    three, four, rest = call(
        functools.partial(p_grads_kernel, 6 * rows),
        [shape((size * rows, width), BF16) for size in (2, 1, 7)],
        smem(1) + vmem(8),
        (temp, *deltas, *q_parts),
    )
    sent = [
        call(q_grads_kernel, shape((part_rows, width), BF16), smem(1) + vmem(2), (temp, delta, p_all))
        for delta in deltas[1:]
    ]
    pair, one, two, own = call(
        local_grads_kernel,
        [shape((size * rows, width), BF16) for size in (2, 2, 2, 4)],
        smem(1) + vmem(9),
        (temp, p_all, *deltas, *q_parts),
    )
    q_terms = scatter_queries([own, *sent], rows)
    p_terms = scatter_passages(pair, one, two, three, four, rest, rows)
    query_grads, passage_grads = (
        call(final_kernel, shape((rows, width), BF16), vmem(1 + len(terms)), (array, *terms))
        for array, terms in ((queries, q_terms), (passages, p_terms))
    )
    return (loss.reshape(rows), query_grads, passage_grads)


def solution(mesh):
    fine = Mesh(mesh.devices.reshape(SIZES), AXES)
    return jax.shard_map(
        local,
        mesh=fine,
        in_specs=(P(AXES, None), P(AXES, None), P(("zl", "core")), P()),
        out_specs=(P(AXES), P(AXES, None), P(AXES, None)),
        check_vma=False,
    )
```
